32 devices in a mesh: inst: 4 (over y, x), space: 8 (over z, core).
Axes of the slice: x: 2, y: 2, z: 4, core: 2. Of those that a mesh axis runs over, the one named last changes fastest.
Arguments:
- field_start: float32 [32, 128, 64, 128], P('inst', 'space'), may hold values from -6 to 6
- source: float32 [32, 128, 64, 128], P('inst', 'space'), may hold values from -6 to 6
- material: int32 [128, 64, 128], P('space'), may hold values from 0 to 7
- face_flags: int32 [32, 3, 128, 64, 128], P('inst', None, 'space'), may hold values from 0 to 1
- disp_table: float32 [8], replicated, may hold values from 0.3 to 3
- perm_table: float32 [8], replicated, may hold values from 0.2 to 2
Outputs:
- residual: float32 [32, 128, 64, 128], P('inst', 'space')
- field: float32 [32, 128, 64, 128], P('inst', 'space')
The draws below stay inside these ranges and needn't reach their ends.
All inputs are finite; a program needn't handle non-finite values.
Results may differ from the reference program's by a relative error of at most 0.00005.
Values sent between devices are 32-bit elements; how exact they have to be, the bound alone decides.
No kernel may reach another device: no remote copies, remote signals or barrier semaphores. Data moves between devices by JAX's collectives and lax.ppermute only.
A program may use at most 192 MiB of HBM per device.

```python
import math
import jax
import jax.numpy as jnp
from jax import lax

NT = 32
NMAT = 8
NX = 64
NY = 128
NZ = 128


def place_ends(entries, rng, low, top_value):
    longest = entries.shape.index(max(entries.shape))
    spots = []
    for shift in (0, 1):
        where = [jax.random.randint(jax.random.fold_in(rng, axis), (), 0, length) for axis, length in enumerate(entries.shape)]
        where[longest] = (where[longest] + shift) % entries.shape[longest]
        spots.append(tuple(where))
    return entries.at[spots[0]].set(low).at[spots[1]].set(top_value)


def shard_levels(stream_key, extent, shards, least, high):
    gain, own = 1.0, jax.random.fold_in(stream_key, 6)
    for axis_at, parts in shards:
        draws = jnp.exp(jax.random.uniform(jax.random.fold_in(own, axis_at), (parts,), jnp.float32, least / len(shards), high / len(shards)))
        gain = gain * jnp.repeat(draws, extent[axis_at] // parts).reshape([-1 if axis == axis_at else 1 for axis in range(len(extent))])
    return gain


def gaussian(stream_key, extent, spread, limit, shards=(), held_as=jnp.bfloat16):
    drawn = spread * jax.random.normal(stream_key, extent, jnp.float32)
    if shards:
        drawn = drawn * shard_levels(stream_key, extent, shards, -0.22, 0.18)
    return jnp.clip(drawn, -limit, limit).astype(held_as)


def setup_inputs(seed: int = 0) -> dict:
    key_list = jax.random.split(jax.random.key(seed), 7)
    field_start = gaussian(key_list[0], (NT, NZ, NX, NY), 1.0, 6.0, ((0, 4), (1, 8)), jnp.float32)
    source = gaussian(key_list[1], (NT, NZ, NX, NY), 1.0, 6.0, ((0, 4), (1, 8)), jnp.float32)
    material = place_ends(jax.random.randint(key_list[2], (NZ, NX, NY), 0, NMAT), jax.random.fold_in(key_list[2], 1), 0, NMAT - 1).astype(jnp.int32)
    face_flags = place_ends(jax.random.randint(key_list[3], (NT, 3, NZ, NX, NY), 0, 2), jax.random.fold_in(key_list[3], 1), 0, 1).astype(jnp.int32)
    disp_table = jnp.clip(jnp.exp(jax.random.uniform(key_list[4], (NMAT,), jnp.float32, math.log(0.3), math.log(3.0))), 0.3, 3.0)
    perm_table = jnp.clip(jnp.exp(jax.random.uniform(key_list[5], (NMAT,), jnp.float32, math.log(0.2), math.log(2.0))), 0.2, 2.0)
    return {"field_start": field_start, "source": source, "material": material, "face_flags": face_flags, "disp_table": disp_table, "perm_table": perm_table}


omega_scale = 0.25
decay_rate = 0.3
relax_weight = 0.8


def spectral_matrix(first, count):
    rows = first + jnp.arange(count)
    cols = jnp.arange(NT)
    diff = rows[:, None] - cols[None, :]
    angle = jnp.pi * diff.astype(jnp.float32) / NT
    parity = 1.0 - 2.0 * (diff % 2).astype(jnp.float32)
    safe = jnp.where(diff == 0, 1.0, jnp.sin(angle))
    return jnp.where(diff == 0, 0.0, 0.5 * parity * jnp.cos(angle) / safe).astype(jnp.float32)


def lookup(material, table):
    total = jnp.zeros(material.shape, jnp.float32)
    for klass in range(table.shape[0]):
        total = total + jnp.where(material == klass, table[klass], 0.0)
    return total


def next_along(field, axis):
    count = field.shape[axis]
    zeros = jnp.zeros_like(lax.slice_in_dim(field, 0, 1, axis=axis))
    return jnp.concatenate([lax.slice_in_dim(field, 1, count, axis=axis), zeros], axis)


def prev_along(field, axis):
    count = field.shape[axis]
    zeros = jnp.zeros_like(lax.slice_in_dim(field, 0, 1, axis=axis))
    return jnp.concatenate([zeros, lax.slice_in_dim(field, 0, count - 1, axis=axis)], axis)


def face_terms(field, up_val, lo_val, kappa, lo_kappa, flow, lo_flow):
    return (kappa * (field - up_val) + lo_kappa * (field - lo_val)
            + jnp.maximum(flow, 0.0) * field + jnp.minimum(flow, 0.0) * up_val
            - jnp.maximum(lo_flow, 0.0) * lo_val - jnp.minimum(lo_flow, 0.0) * field)


def diag_terms(kappa, lo_kappa, flow, lo_flow):
    return kappa + lo_kappa + jnp.maximum(flow, 0.0) - jnp.minimum(lo_flow, 0.0)


def reference(field_start, source, material, face_flags, disp_table, perm_table):
    kappa = lookup(material, disp_table)
    speed = lookup(material, perm_table)
    moments = jnp.arange(NT).astype(jnp.float32)
    tide = 1.0 + 0.5 * jnp.cos(2.0 * jnp.pi * moments / NT)
    dmat = spectral_matrix(0, NT)

    def local(args):
        field_now, flags_now, tide_now = args
        flow = speed[None] * tide_now * (1.0 - 2.0 * flags_now.astype(jnp.float32))
        total = decay_rate * field_now
        diag = decay_rate + jnp.zeros_like(field_now)
        for axis in range(3):
            total = total + face_terms(field_now, next_along(field_now, axis), prev_along(field_now, axis),
                                       kappa, prev_along(kappa, axis), flow[axis], prev_along(flow[axis], axis))
            diag = diag + diag_terms(kappa, prev_along(kappa, axis), flow[axis], prev_along(flow[axis], axis))
        return total, diag

    def residual_of(field):
        coupled = jnp.einsum("ts,szxy->tzxy", dmat, field, precision=lax.Precision.HIGHEST)
        stencil, diag = lax.map(local, (field, face_flags, tide))
        return omega_scale * coupled + stencil - source, diag

    residual, diag = residual_of(field_start)
    middle = field_start - relax_weight * residual / diag
    second, unused = residual_of(middle)
    field = middle - relax_weight * second / diag
    return residual, field
```

```python
import functools

import jax
import jax.numpy as jnp
from jax import lax
from jax.experimental import pallas as pl
from jax.experimental.pallas import tpu as pltpu
from jax.sharding import PartitionSpec as P

NT = 32


omega_scale = 0.25
decay_rate = 0.3
relax_weight = 0.8

CHUNKS = 2
SUB = 8
MIB = 1 << 20


def spectral_blocks(me, n, count):
    spots = jnp.arange(NT)
    moments = (me ^ (spots // count)) * count + spots % count
    diff = moments[:, None] - moments[None, :]
    angle = jnp.pi * diff.astype(jnp.float32) / NT
    parity = 1.0 - 2.0 * (diff % 2).astype(jnp.float32)
    safe = jnp.where(diff == 0, 1.0, jnp.sin(angle))
    dmat = omega_scale * jnp.where(diff == 0, 0.0, 0.5 * parity * jnp.cos(angle) / safe)
    rows = jnp.repeat(jnp.repeat(dmat, SUB, 0), SUB, 1)
    lane = jnp.arange(NT * SUB) % SUB
    return jnp.where(lane[:, None] == lane[None, :], rows, 0.0)


def prep_kernel(disp_ref, perm_ref, tide_ref, material_ref, flags_ref, kappa_ref, speed_ref, top_ref):
    depth = material_ref.shape[0]

    def layer(z, carry):
        material = material_ref[z]
        kappa = jnp.zeros(material.shape, jnp.float32)
        speed = jnp.zeros(material.shape, jnp.float32)
        for klass in range(disp_ref.shape[0]):
            here = material == klass
            kappa = jnp.where(here, disp_ref[klass], kappa)
            speed = jnp.where(here, perm_ref[klass], speed)
        kappa_ref[z] = kappa
        speed_ref[z] = speed
        return carry

    lax.fori_loop(0, depth, layer, 0)
    top_ref[0] = kappa_ref[depth - 1]
    for t in range(flags_ref.shape[0]):
        flow = speed_ref[depth - 1] * tide_ref[t]
        top_ref[t + 1] = jnp.where(flags_ref[t, 0, 0] != 0, -flow, flow)


def prep(disp_table, perm_table, tide, material, face_flags):
    count, _, depth, width, length = face_flags.shape
    smem = pl.BlockSpec(memory_space=pltpu.SMEM)
    cells = pl.BlockSpec((depth, width, length), lambda i: (0, 0, 0))
    return pl.pallas_call(
        prep_kernel,
        grid=(1,),
        in_specs=[
            smem,
            smem,
            smem,
            cells,
            pl.BlockSpec((count, 1, 1, width, length), lambda i: (0, 0, depth - 1, 0, 0)),
        ],
        out_specs=[cells, cells, pl.BlockSpec((count + 1, width, length), lambda i: (0, 0, 0))],
        out_shape=[
            jax.ShapeDtypeStruct(material.shape, jnp.float32),
            jax.ShapeDtypeStruct(material.shape, jnp.float32),
            jax.ShapeDtypeStruct((count + 1, width, length), jnp.float32),
        ],
        compiler_params=pltpu.CompilerParams(vmem_limit_bytes=16 * MIB),
        cost_estimate=pl.CostEstimate(flops=material.size * 30, bytes_accessed=material.size * 12, transcendentals=0),
        name="prep",
    )(disp_table, perm_table, tide, material, face_flags)


def stencil_kernel(second, tide_ref, u_ref, low_ref, high_ref, flags_ref, src_ref, kappa_ref, speed_ref, below_k_ref, below_f_ref, *rest):
    if second:
        winv_ref, out_ref = rest
    else:
        out_ref, winv_ref = rest
    depth, width, length = u_ref.shape[1:]
    tide = tide_ref[pl.program_id(0)]
    row = lax.broadcasted_iota(jnp.int32, (width, length), 0)
    col = lax.broadcasted_iota(jnp.int32, (width, length), 1)
    last_row, last_col = row == width - 1, col == length - 1

    below_k, below_f = below_k_ref[0], below_f_ref[0]
    au_low = (below_k + jnp.maximum(below_f, 0.0)) * low_ref[0, 0]
    b_low = below_k - jnp.minimum(below_f, 0.0)

    def layer(z, carry, u_up):
        au_low, b_low = carry
        u = u_ref[0, z]
        kappa = kappa_ref[z]
        full = kappa + speed_ref[z] * tide

        def coefs(dim):
            back = flags_ref[0, dim, z] != 0
            return jnp.where(back, kappa, full), jnp.where(back, full, kappa)

        a, b = coefs(0)
        total = b * u_up + au_low
        diag = (decay_rate + a) + b_low
        next_carry = (a * u, b)
        for dim, last in ((1, last_row), (2, last_col)):
            a, b = coefs(dim)
            size = u.shape[dim - 1]
            b = jnp.where(last, 0.0, b)
            au = jnp.where(last, 0.0, a * u)
            total = total + b * pltpu.roll(u, size - 1, dim - 1) + pltpu.roll(au, 1, dim - 1)
            if not second:
                diag = diag + (a + pltpu.roll(b, 1, dim - 1))
        if second:
            out_ref[0, z] = (1.0 - relax_weight) * u + winv_ref[0, z] * (total + src_ref[0, z])
        else:
            out_ref[0, z] = diag * u - total - src_ref[0, z]
            winv_ref[0, z] = relax_weight / diag
        return next_carry

    carry = lax.fori_loop(0, depth - 1, lambda z, c: layer(z, c, u_ref[0, z + 1]), (au_low, b_low))
    layer(depth - 1, carry, high_ref[0, 0])


def stencil(second, tide, u, low, high, flags, src, kappa, speed, below, winv=None):
    count, depth, width, length = u.shape
    field = pl.BlockSpec((1, depth, width, length), lambda t: (t, 0, 0, 0))
    plane = pl.BlockSpec((1, 1, width, length), lambda t: (t, 0, 0, 0))
    cells = pl.BlockSpec((depth, width, length), lambda t: (0, 0, 0))
    in_specs = [
        pl.BlockSpec(memory_space=pltpu.SMEM),
        field,
        plane,
        plane,
        pl.BlockSpec((1, 3, depth, width, length), lambda t: (t, 0, 0, 0, 0)),
        field,
        cells,
        cells,
        pl.BlockSpec((1, width, length), lambda t: (0, 0, 0)),
        pl.BlockSpec((1, width, length), lambda t: (t + 1, 0, 0)),
    ]
    args = [tide, u, low, high, flags, src, kappa, speed, below, below]
    if second:
        in_specs.append(field)
        args.append(winv)
    shape = jax.ShapeDtypeStruct(u.shape, jnp.float32)
    return pl.pallas_call(
        functools.partial(stencil_kernel, second),
        grid=(count,),
        in_specs=in_specs,
        out_specs=field if second else [field, field],
        out_shape=shape if second else [shape, shape],
        compiler_params=pltpu.CompilerParams(vmem_limit_bytes=24 * MIB),
        cost_estimate=pl.CostEstimate(flops=u.size * 60, bytes_accessed=u.size * 28, transcendentals=0),
        name="stencil_two" if second else "stencil_one",
    )(*args)


def apply_kernel(n, me_ref, own_ref, *refs):
    received, mat_ref, outs = refs[: n - 1], refs[n - 1], refs[n:]
    parts = [own_ref, *received]
    count, _, width, length = own_ref.shape
    groups = width // SUB
    blocks = jnp.concatenate([part[:, 0] for part in parts], 0)
    wide = jnp.concatenate(
        [blocks[:, g * SUB : (g + 1) * SUB].reshape(NT * SUB, length) for g in range(groups)], 1
    )
    product = lax.dot_general(
        mat_ref[...],
        wide,
        (((1,), (0,)), ((), ())),
        precision=lax.Precision.HIGHEST,
        preferred_element_type=jnp.float32,
    )
    for g in range(groups):
        piece = product[:, g * length : (g + 1) * length].reshape(NT, SUB, length)
        for m, out in enumerate(outs):
            out[:, 0, g * SUB : (g + 1) * SUB] = piece[m * count : (m + 1) * count]


def apply_time(me, field, received, mat, chunk):
    n = len(received) + 1
    count, depth, width, length = field.shape
    part = received[0].shape[1]
    piece = pl.BlockSpec((count, 1, width, length), lambda i, me: (0, i, 0, 0))
    shape = jax.ShapeDtypeStruct(received[0].shape, jnp.float32)
    size = n * received[0].size
    return pl.pallas_call(
        functools.partial(apply_kernel, n),
        grid_spec=pltpu.PrefetchScalarGridSpec(
            num_scalar_prefetch=1,
            grid=(part,),
            in_specs=[
                pl.BlockSpec((count, 1, width, length), lambda i, me: (0, (chunk * n + me[0]) * part + i, 0, 0)),
                *([piece] * (n - 1)),
                pl.BlockSpec(mat.shape, lambda i, me: (0, 0)),
            ],
            out_specs=[piece] * n,
        ),
        out_shape=[shape] * n,
        compiler_params=pltpu.CompilerParams(vmem_limit_bytes=24 * MIB),
        cost_estimate=pl.CostEstimate(flops=size * 2 * NT * SUB * 6, bytes_accessed=size * 8, transcendentals=0),
        name="apply_time",
    )(me, field, *received, mat)


ROWS = 16


def first_kernel(n, aliased, me_ref, *refs):
    pieces, (s_ref, winv_ref, u_ref) = refs[:n], refs[n : n + 3]
    res_ref, mid_ref, *sends = refs[n + 3 + aliased :]
    part = pieces[0].shape[1]
    for m, piece in enumerate(pieces):
        for i in range(part):
            z = (me_ref[0] ^ m) * part + i
            res = s_ref[:, z] + piece[:, i]
            mid = u_ref[:, z] - winv_ref[:, z] * res
            res_ref[:, z] = res
            mid_ref[:, z] = mid
            if m:
                sends[m - 1][:, i] = mid


def first_update(me, pieces, s, winv, u, chunk, before):
    n = len(pieces)
    count, depth, width, length = u.shape
    part = pieces[0].shape[1]
    piece = pl.BlockSpec((count, part, ROWS, length), lambda i, me: (0, 0, i, 0))
    layers = pl.BlockSpec((count, n * part, ROWS, length), lambda i, me: (0, chunk, i, 0))
    whole = jax.ShapeDtypeStruct(u.shape, jnp.float32)
    aliased = len(before)
    size = n * pieces[0].size
    return pl.pallas_call(
        functools.partial(first_kernel, n, aliased),
        grid_spec=pltpu.PrefetchScalarGridSpec(
            num_scalar_prefetch=1,
            grid=(width // ROWS,),
            in_specs=[piece] * n + [layers] * 3 + [pl.BlockSpec(memory_space=pl.ANY)] * aliased,
            out_specs=[layers] * 2 + [piece] * (n - 1),
        ),
        out_shape=[whole] * 2 + [jax.ShapeDtypeStruct(pieces[0].shape, jnp.float32)] * (n - 1),
        input_output_aliases={n + 4 + i: i for i in range(aliased)},
        compiler_params=pltpu.CompilerParams(vmem_limit_bytes=24 * MIB),
        cost_estimate=pl.CostEstimate(flops=size * 3, bytes_accessed=size * 28, transcendentals=0),
        name="first_update",
    )(me, *pieces, s, winv, u, *before)


def last_kernel(n, aliased, me_ref, *refs):
    pieces, (f_ref, winv_ref) = refs[:n], refs[n : n + 2]
    out_ref = refs[n + 2 + aliased]
    part = pieces[0].shape[1]
    for m, piece in enumerate(pieces):
        for i in range(part):
            z = (me_ref[0] ^ m) * part + i
            out_ref[:, z] = f_ref[:, z] - winv_ref[:, z] * piece[:, i]


def last_update(me, pieces, f, winv, chunk, before):
    n = len(pieces)
    count, depth, width, length = f.shape
    part = pieces[0].shape[1]
    piece = pl.BlockSpec((count, part, ROWS, length), lambda i, me: (0, 0, i, 0))
    layers = pl.BlockSpec((count, n * part, ROWS, length), lambda i, me: (0, chunk, i, 0))
    aliased = len(before)
    size = n * pieces[0].size
    return pl.pallas_call(
        functools.partial(last_kernel, n, aliased),
        grid_spec=pltpu.PrefetchScalarGridSpec(
            num_scalar_prefetch=1,
            grid=(width // ROWS,),
            in_specs=[piece] * n + [layers] * 2 + [pl.BlockSpec(memory_space=pl.ANY)] * aliased,
            out_specs=layers,
        ),
        out_shape=jax.ShapeDtypeStruct(f.shape, jnp.float32),
        input_output_aliases={n + 3: 0} if aliased else {},
        compiler_params=pltpu.CompilerParams(vmem_limit_bytes=24 * MIB),
        cost_estimate=pl.CostEstimate(flops=size * 2, bytes_accessed=size * 16, transcendentals=0),
        name="last_update",
    )(me, *pieces, f, winv, *before)


def exchange(pieces):
    n = len(pieces) + 1
    return [
        lax.ppermute(piece, "inst", [(i, i ^ m) for i in range(n)]) for m, piece in enumerate(pieces, 1)
    ]


def halos(field):
    slabs = lax.axis_size("space")
    upward = [(i, i + 1) for i in range(slabs - 1)]
    downward = [(i + 1, i) for i in range(slabs - 1)]
    return lax.ppermute(field[:, -1:], "space", upward), lax.ppermute(field[:, :1], "space", downward)


def body(field_start, source, material, face_flags, disp_table, perm_table):
    count, depth, width, length = field_start.shape
    n = lax.axis_size("inst")
    slabs = lax.axis_size("space")
    chunks = min(CHUNKS, depth // n)
    part = depth // (chunks * n)
    me = lax.axis_index("inst")
    me_array = me.reshape(1).astype(jnp.int32)

    going = [
        [
            lax.dynamic_slice_in_dim(field_start, (chunk * n + (me ^ m)) * part, part, axis=1)
            for m in range(1, n)
        ]
        for chunk in range(chunks)
    ]
    there = [exchange(pieces) for pieces in going]

    moments = (me * count + jnp.arange(count)).astype(jnp.float32)
    tide = 1.0 + 0.5 * jnp.cos(2.0 * jnp.pi * moments / NT)
    mat = spectral_blocks(me, n, count)
    kappa, speed, top = prep(disp_table, perm_table, tide, material, face_flags)
    below = lax.ppermute(top, "space", [(i, i + 1) for i in range(slabs - 1)])
    low, high = halos(field_start)
    plain, winv = stencil(False, tide, field_start, low, high, face_flags, source, kappa, speed, below)

    back = []
    for chunk in range(chunks):
        own, *rest = apply_time(me_array, field_start, there[chunk], mat, chunk)
        back.append([own] + exchange(rest))

    whole = []
    there = []
    for chunk in range(chunks):
        *whole, = first_update(me_array, back[chunk], plain, winv, field_start, chunk, whole)
        whole, sends = whole[:2], whole[2:]
        there.append(exchange(sends))
    residual, middle = whole

    low, high = halos(middle)
    base = stencil(True, tide, middle, low, high, face_flags, source, kappa, speed, below, winv)

    back = []
    for chunk in range(chunks):
        own, *rest = apply_time(me_array, middle, there[chunk], mat, chunk)
        back.append([own] + exchange(rest))

    field = []
    for chunk in range(chunks):
        field = [last_update(me_array, back[chunk], base, winv, chunk, field)]
    return (residual, field[0])


def solution(mesh):
    return jax.shard_map(
        body,
        mesh=mesh,
        in_specs=(
            P("inst", "space", None, None),
            P("inst", "space", None, None),
            P("space", None, None),
            P("inst", None, "space", None, None),
            P(),
            P(),
        ),
        out_specs=(P("inst", "space", None, None), P("inst", "space", None, None)),
        check_vma=False,
    )
```

```python
import functools

import jax
import jax.numpy as jnp
from jax import lax
from jax.experimental import pallas as pl
from jax.experimental.pallas import tpu as pltpu
from jax.sharding import PartitionSpec as P

NT = 32


omega_scale = 0.25
decay_rate = 0.3
relax_weight = 0.8

CHUNKS = 2
PARTS = 2
SUB = 8
VMEM = 20 << 20
COST = pl.CostEstimate(flops=1 << 10, bytes_accessed=1 << 10, transcendentals=0)


def spectral_blocks(me, n, count):
    spots = jnp.arange(NT)
    moments = (me ^ (spots // count)) * count + spots % count
    diff = moments[:, None] - moments[None, :]
    angle = jnp.pi * diff.astype(jnp.float32) / NT
    parity = 1.0 - 2.0 * (diff % 2).astype(jnp.float32)
    safe = jnp.where(diff == 0, 1.0, jnp.sin(angle))
    dmat = omega_scale * jnp.where(diff == 0, 0.0, 0.5 * parity * jnp.cos(angle) / safe)
    rows = jnp.repeat(jnp.repeat(dmat, SUB, 0), SUB, 1)
    lane = jnp.arange(NT * SUB) % SUB
    return jnp.where(lane[:, None] == lane[None, :], rows, 0.0)


def in_hbm(*arrays):
    return [pltpu.with_memory_space_constraint(array, pltpu.HBM) for array in arrays]


def cut_kernel(me_ref, *refs):
    half = len(refs) // 2
    for source, out in zip(refs[:half], refs[half:]):
        out[...] = source[...]


def cut(me, field, n, chunk, part):
    count, depth, width, length = field.shape

    def block(m):
        return pl.BlockSpec(
            (count, 1, width, length), lambda i, me: (0, (chunk * n + (me[0] ^ m)) * part + i, 0, 0)
        )

    piece = pl.BlockSpec((count, 1, width, length), lambda i, me: (0, i, 0, 0))
    return pl.pallas_call(
        cut_kernel,
        grid_spec=pltpu.PrefetchScalarGridSpec(
            num_scalar_prefetch=1,
            grid=(part,),
            in_specs=[block(m) for m in range(1, n)],
            out_specs=[piece] * (n - 1),
        ),
        out_shape=[jax.ShapeDtypeStruct((count, part, width, length), jnp.float32)] * (n - 1),
        compiler_params=pltpu.CompilerParams(vmem_limit_bytes=VMEM),
        cost_estimate=COST,
        name="cut",
    )(me, *in_hbm(*[field] * (n - 1)))


def prep_kernel(
    disp_ref, perm_ref, tide_ref, material_ref, flags_ref, bottom_ref, last_ref, kappa_ref, speed_ref, up_ref, down_ref
):
    depth = material_ref.shape[0]
    count = flags_ref.shape[0]

    def layer(z, carry):
        material = material_ref[z]
        kappa = jnp.zeros(material.shape, jnp.float32)
        speed = jnp.zeros(material.shape, jnp.float32)
        for klass in range(disp_ref.shape[0]):
            here = material == klass
            kappa = jnp.where(here, disp_ref[klass], kappa)
            speed = jnp.where(here, perm_ref[klass], speed)
        kappa_ref[z] = kappa
        speed_ref[z] = speed
        return carry

    lax.fori_loop(0, depth, layer, 0)
    up_ref[2 * count] = kappa_ref[depth - 1]
    for t in range(count):
        flow = speed_ref[depth - 1] * tide_ref[t]
        up_ref[t] = last_ref[t, 0]
        up_ref[count + t] = jnp.where(flags_ref[t, 0, 0] != 0, -flow, flow)
        down_ref[t] = bottom_ref[t, 0]


def prep(disp_table, perm_table, tide, material, face_flags, field):
    count, _, depth, width, length = face_flags.shape
    smem = pl.BlockSpec(memory_space=pltpu.SMEM)
    cells = pl.BlockSpec((depth, width, length), lambda i: (0, 0, 0))
    up = (2 * count + 1, width, length)
    down = (count, width, length)
    return pl.pallas_call(
        prep_kernel,
        grid=(1,),
        in_specs=[
            smem,
            smem,
            smem,
            cells,
            pl.BlockSpec((count, 1, 1, width, length), lambda i: (0, 0, depth - 1, 0, 0)),
            pl.BlockSpec((count, 1, width, length), lambda i: (0, 0, 0, 0)),
            pl.BlockSpec((count, 1, width, length), lambda i: (0, depth - 1, 0, 0)),
        ],
        out_specs=[
            cells,
            cells,
            pl.BlockSpec(up, lambda i: (0, 0, 0)),
            pl.BlockSpec(down, lambda i: (0, 0, 0)),
        ],
        out_shape=[
            jax.ShapeDtypeStruct(material.shape, jnp.float32),
            jax.ShapeDtypeStruct(material.shape, jnp.float32),
            jax.ShapeDtypeStruct(up, jnp.float32),
            jax.ShapeDtypeStruct(down, jnp.float32),
        ],
        compiler_params=pltpu.CompilerParams(vmem_limit_bytes=VMEM),
        cost_estimate=COST,
        name="prep",
    )(disp_table, perm_table, tide, *in_hbm(material, face_flags, field, field))


def stencil_kernel(
    second, first, aliased, tide_ref, u_ref, low_ref, high_ref, flags_ref, src_ref, kappa_ref, speed_ref, below_k_ref, below_f_ref, *rest
):
    if second:
        winv_ref, out_ref = rest[0], rest[-1]
    else:
        out_ref, winv_ref = rest[aliased:]
    depth, width, length = u_ref.shape[1:]
    tide = tide_ref[first + pl.program_id(0)]
    row = lax.broadcasted_iota(jnp.int32, (width, length), 0)
    col = lax.broadcasted_iota(jnp.int32, (width, length), 1)
    last_row, last_col = row == width - 1, col == length - 1

    below_k, below_f = below_k_ref[0], below_f_ref[0]
    au_low = (below_k + jnp.maximum(below_f, 0.0)) * low_ref[0]
    b_low = below_k - jnp.minimum(below_f, 0.0)

    def layer(z, carry, u_up):
        au_low, b_low = carry
        u = u_ref[0, z]
        kappa = kappa_ref[z]
        full = kappa + speed_ref[z] * tide

        def coefs(dim):
            back = flags_ref[0, dim, z] != 0
            return jnp.where(back, kappa, full), jnp.where(back, full, kappa)

        a, b = coefs(0)
        total = b * u_up + au_low
        diag = (decay_rate + a) + b_low
        next_carry = (a * u, b)
        for dim, last in ((1, last_row), (2, last_col)):
            a, b = coefs(dim)
            size = u.shape[dim - 1]
            b = jnp.where(last, 0.0, b)
            au = jnp.where(last, 0.0, a * u)
            total = total + b * pltpu.roll(u, size - 1, dim - 1) + pltpu.roll(au, 1, dim - 1)
            if not second:
                diag = diag + (a + pltpu.roll(b, 1, dim - 1))
        if second:
            out_ref[0, z] = (1.0 - relax_weight) * u + winv_ref[0, z] * (total + src_ref[0, z])
        else:
            out_ref[0, z] = diag * u - total - src_ref[0, z]
            winv_ref[0, z] = relax_weight / diag
        return next_carry

    carry = lax.fori_loop(0, depth - 1, lambda z, c: layer(z, c, u_ref[0, z + 1]), (au_low, b_low))
    layer(depth - 1, carry, high_ref[0])


def stencil(second, part, tide, u, low, high, flags, src, kappa, speed, below, winv=None, before=()):
    count, depth, width, length = u.shape
    first, stop = count * part // PARTS, count * (part + 1) // PARTS
    field = pl.BlockSpec((1, depth, width, length), lambda t: (first + t, 0, 0, 0))
    plane = pl.BlockSpec((1, width, length), lambda t: (first + t, 0, 0))
    cells = pl.BlockSpec((depth, width, length), lambda t: (0, 0, 0))
    in_specs = [
        pl.BlockSpec(memory_space=pltpu.SMEM),
        field,
        plane,
        plane,
        pl.BlockSpec((1, 3, depth, width, length), lambda t: (first + t, 0, 0, 0, 0)),
        field,
        cells,
        cells,
        pl.BlockSpec((1, width, length), lambda t: (2 * count, 0, 0)),
        pl.BlockSpec((1, width, length), lambda t: (count + first + t, 0, 0)),
    ]
    args = [tide, *in_hbm(u), low, high, *in_hbm(flags, src), kappa, speed, below, below]
    if second:
        in_specs.append(field)
        args.extend(in_hbm(winv))
    aliases = {len(args) + i: i for i in range(len(before))}
    in_specs += [pl.BlockSpec(memory_space=pl.ANY)] * len(before)
    args.extend(in_hbm(*before))
    shape = pltpu.HBM(u.shape, jnp.float32)
    outs = 1 if second else 2
    return pl.pallas_call(
        functools.partial(stencil_kernel, second, first, len(before)),
        grid=(stop - first,),
        in_specs=in_specs,
        out_specs=[field] * outs,
        out_shape=[shape] * outs,
        input_output_aliases=aliases,
        compiler_params=pltpu.CompilerParams(vmem_limit_bytes=VMEM),
        cost_estimate=COST,
        name="stencil_two" if second else "stencil_one",
    )(*args)


def apply_kernel(n, me_ref, own_ref, *refs):
    received, mat_ref, outs = refs[: n - 1], refs[n - 1], refs[n:]
    parts = [own_ref, *received]
    count, _, width, length = own_ref.shape
    groups = width // SUB
    blocks = jnp.concatenate([part[:, 0] for part in parts], 0)
    wide = jnp.concatenate(
        [blocks[:, g * SUB : (g + 1) * SUB].reshape(NT * SUB, length) for g in range(groups)], 1
    )
    product = lax.dot_general(
        mat_ref[...],
        wide,
        (((1,), (0,)), ((), ())),
        precision=lax.Precision.HIGHEST,
        preferred_element_type=jnp.float32,
    )
    for g in range(groups):
        piece = product[:, g * length : (g + 1) * length].reshape(NT, SUB, length)
        for m, out in enumerate(outs):
            out[:, 0, g * SUB : (g + 1) * SUB] = piece[m * count : (m + 1) * count]


def apply_time(me, field, received, mat, chunk):
    n = len(received) + 1
    count, depth, width, length = field.shape
    part = received[0].shape[1]
    piece = pl.BlockSpec((count, 1, width, length), lambda i, me: (0, i, 0, 0))
    shape = jax.ShapeDtypeStruct(received[0].shape, jnp.float32)
    size = n * received[0].size
    return pl.pallas_call(
        functools.partial(apply_kernel, n),
        grid_spec=pltpu.PrefetchScalarGridSpec(
            num_scalar_prefetch=1,
            grid=(part,),
            in_specs=[
                pl.BlockSpec((count, 1, width, length), lambda i, me: (0, (chunk * n + me[0]) * part + i, 0, 0)),
                *([piece] * (n - 1)),
                pl.BlockSpec(mat.shape, lambda i, me: (0, 0)),
            ],
            out_specs=[piece] * n,
        ),
        out_shape=[shape] * n,
        compiler_params=pltpu.CompilerParams(vmem_limit_bytes=VMEM),
        cost_estimate=COST,
        name="apply_time",
    )(me, *in_hbm(field), *received, mat)


ROWS = 16


def first_kernel(n, aliased, me_ref, *refs):
    pieces, (s_ref, winv_ref, u_ref) = refs[:n], refs[n : n + 3]
    res_ref, mid_ref, first_ref, last_ref, *sends = refs[n + 3 + aliased :]
    part = pieces[0].shape[1]
    for m, piece in enumerate(pieces):
        for i in range(part):
            z = (me_ref[0] ^ m) * part + i
            res = s_ref[:, z] + piece[:, i]
            mid = u_ref[:, z] - winv_ref[:, z] * res
            res_ref[:, z] = res
            mid_ref[:, z] = mid
            if m:
                sends[m - 1][:, i] = mid
    first_ref[...] = mid_ref[:, 0]
    last_ref[...] = mid_ref[:, n * part - 1]


def first_update(me, pieces, s, winv, u, chunk, before):
    n = len(pieces)
    count, depth, width, length = u.shape
    part = pieces[0].shape[1]
    piece = pl.BlockSpec((count, part, ROWS, length), lambda i, me: (0, 0, i, 0))
    layers = pl.BlockSpec((count, n * part, ROWS, length), lambda i, me: (0, chunk, i, 0))
    whole = pltpu.HBM(u.shape, jnp.float32)
    aliased = len(before)
    size = n * pieces[0].size
    return pl.pallas_call(
        functools.partial(first_kernel, n, aliased),
        grid_spec=pltpu.PrefetchScalarGridSpec(
            num_scalar_prefetch=1,
            grid=(width // ROWS,),
            in_specs=[piece] * n + [layers] * 3 + [pl.BlockSpec(memory_space=pl.ANY)] * aliased,
            out_specs=[layers] * 2 + [pl.BlockSpec((count, ROWS, length), lambda i, me: (0, i, 0))] * 2 + [piece] * (n - 1),
        ),
        out_shape=[whole] * 2
        + [jax.ShapeDtypeStruct((count, width, length), jnp.float32)] * 2
        + [jax.ShapeDtypeStruct(pieces[0].shape, jnp.float32)] * (n - 1),
        input_output_aliases={n + 4 + i: i for i in range(aliased)},
        compiler_params=pltpu.CompilerParams(vmem_limit_bytes=VMEM),
        cost_estimate=COST,
        name="first_update",
    )(me, *pieces, *in_hbm(s, winv, u, *before))


def last_kernel(piece_ref, base_ref, winv_ref, *refs):
    refs[-1][...] = base_ref[...] - winv_ref[...] * piece_ref[...]


def last_update(spot, piece, base, winv, before):
    count, part, width, length = piece.shape
    layers = pl.BlockSpec((count, 1, width, length), lambda i, spot: (0, spot[0] * part + i, 0, 0))
    aliased = len(before)
    return pl.pallas_call(
        lambda spot_ref, *refs: last_kernel(*refs),
        grid_spec=pltpu.PrefetchScalarGridSpec(
            num_scalar_prefetch=1,
            grid=(part,),
            in_specs=[pl.BlockSpec((count, 1, width, length), lambda i, spot: (0, i, 0, 0)), layers, layers]
            + [pl.BlockSpec(memory_space=pl.ANY)] * aliased,
            out_specs=layers,
        ),
        out_shape=pltpu.HBM(base.shape, jnp.float32),
        input_output_aliases={4: 0} if aliased else {},
        compiler_params=pltpu.CompilerParams(vmem_limit_bytes=VMEM),
        cost_estimate=COST,
        name="last_update",
    )(spot, piece, *in_hbm(base, winv, *before))


def exchange(pieces):
    n = len(pieces) + 1
    return [
        lax.ppermute(piece, "inst", [(i, i ^ m) for i in range(n)]) for m, piece in enumerate(pieces, 1)
    ]


def after(arrays, *first):
    return lax.optimization_barrier((arrays, first))[0]


def upward(plane):
    return lax.ppermute(plane, "space", [(i, i + 1) for i in range(lax.axis_size("space") - 1)])


def downward(plane):
    return lax.ppermute(plane, "space", [(i + 1, i) for i in range(lax.axis_size("space") - 1)])


def body(field_start, source, material, face_flags, disp_table, perm_table):
    count, depth, width, length = field_start.shape
    n = lax.axis_size("inst")
    chunks = min(CHUNKS, depth // n)
    part = depth // (chunks * n)
    me = lax.axis_index("inst")
    me_array = me.reshape(1).astype(jnp.int32)

    going = cut(me_array, field_start, n, 0, part)
    there = [exchange(going)]
    start, flags, material = after((field_start, face_flags, material), *going)

    moments = (me * count + jnp.arange(count)).astype(jnp.float32)
    tide = 1.0 + 0.5 * jnp.cos(2.0 * jnp.pi * moments / NT)
    mat = spectral_blocks(me, n, count)
    kappa, speed, up, down = prep(disp_table, perm_table, tide, material, flags, start)
    below, high = upward(up), downward(down)
    start = after(start, below, high)
    for chunk in range(1, chunks):
        going = cut(me_array, start, n, chunk, part)
        there.append(exchange(going))
        start = after(start, *going)
    shared = (below, high, flags, source, kappa, speed, below)
    first = stencil(False, 0, tide, start, *shared)

    back = []
    there[0] = after(there[0], first)
    for chunk in range(chunks):
        own, *rest = apply_time(me_array, field_start, there[chunk], mat, chunk)
        back.append([own] + exchange(rest))
    for half in range(1, PARTS):
        first = stencil(False, half, tide, after(field_start, back[0][1]), *shared, before=first)
    plain, winv = first

    whole = []
    there = []
    low = high = None
    for chunk in range(chunks):
        if chunk:
            back[chunk] = after(back[chunk], high)
        done = first_update(me_array, back[chunk], plain, winv, field_start, chunk, whole)
        whole, (bottom, last), sends = done[:2], done[2:4], done[4:]
        if chunk == 0:
            high = downward(bottom)
        if chunk == chunks - 1:
            low = upward(last)
        there.append(exchange(sends))
    residual, middle = whole
    there[0] = after(there[0], low)

    back = []
    second = ()
    for chunk in range(chunks):
        own, *rest = apply_time(me_array, middle, there[chunk], mat, chunk)
        back.append([own] + exchange(rest))
        if chunk < PARTS:
            ready = there[1][0] if chunk == 0 else back[0][1]
            now = after(middle, ready)
            second = stencil(True, chunk, tide, now, low, high, face_flags, source, kappa, speed, below, winv, second)
            if chunk == 0:
                there[1] = after(there[1], *second)
    base = second[0]

    field = []
    for chunk in range(chunks):
        for m, piece in enumerate(back[chunk]):
            spot = (chunk * n + (me ^ m)).reshape(1).astype(jnp.int32)
            field = [last_update(spot, piece, base, winv, field)]
    return (residual, field[0])


def solution(mesh):
    return jax.shard_map(
        body,
        mesh=mesh,
        in_specs=(
            P("inst", "space", None, None),
            P("inst", "space", None, None),
            P("space", None, None),
            P("inst", None, "space", None, None),
            P(),
            P(),
        ),
        out_specs=(P("inst", "space", None, None), P("inst", "space", None, None)),
        check_vma=False,
    )
```

```python
import functools

import jax
import jax.numpy as jnp
from jax import lax
from jax.experimental import pallas as pl
from jax.experimental.pallas import tpu as pltpu
from jax.sharding import PartitionSpec as P

NT = 32


omega_scale = 0.25
decay_rate = 0.3
relax_weight = 0.8

CHUNKS = 2
PARTS = 2
SUB = 8
VMEM = 20 << 20
COST = pl.CostEstimate(flops=1 << 10, bytes_accessed=1 << 10, transcendentals=0)


def spectral_blocks(me, n, count):
    spots = jnp.arange(NT)
    moments = (me ^ (spots // count)) * count + spots % count
    diff = moments[:, None] - moments[None, :]
    angle = jnp.pi * diff.astype(jnp.float32) / NT
    parity = 1.0 - 2.0 * (diff % 2).astype(jnp.float32)
    safe = jnp.where(diff == 0, 1.0, jnp.sin(angle))
    dmat = omega_scale * jnp.where(diff == 0, 0.0, 0.5 * parity * jnp.cos(angle) / safe)
    rows = jnp.repeat(jnp.repeat(dmat, SUB, 0), SUB, 1)
    lane = jnp.arange(NT * SUB) % SUB
    return jnp.where(lane[:, None] == lane[None, :], rows, 0.0)


def in_hbm(*arrays):
    return [pltpu.with_memory_space_constraint(array, pltpu.HBM) for array in arrays]


def cut_kernel(me_ref, *refs):
    half = len(refs) // 2
    for source, out in zip(refs[:half], refs[half:]):
        out[...] = source[...]


def cut(me, field, n, chunk, part, partners=None):
    count, depth, width, length = field.shape
    partners = range(1, n) if partners is None else partners

    def block(m):
        return pl.BlockSpec(
            (count, 1, width, length), lambda i, me: (0, (chunk * n + (me[0] ^ m)) * part + i, 0, 0)
        )

    piece = pl.BlockSpec((count, 1, width, length), lambda i, me: (0, i, 0, 0))
    return pl.pallas_call(
        cut_kernel,
        grid_spec=pltpu.PrefetchScalarGridSpec(
            num_scalar_prefetch=1,
            grid=(part,),
            in_specs=[block(m) for m in partners],
            out_specs=[piece] * len(partners),
        ),
        out_shape=[jax.ShapeDtypeStruct((count, part, width, length), jnp.float32)] * len(partners),
        compiler_params=pltpu.CompilerParams(vmem_limit_bytes=VMEM),
        cost_estimate=COST,
        name="cut",
    )(me, *in_hbm(*[field] * len(partners)))


def prep_kernel(
    disp_ref, perm_ref, tide_ref, material_ref, flags_ref, bottom_ref, last_ref, kappa_ref, speed_ref, up_ref, down_ref
):
    depth = material_ref.shape[0]
    count = flags_ref.shape[0]

    def layer(z, carry):
        material = material_ref[z]
        kappa = jnp.zeros(material.shape, jnp.float32)
        speed = jnp.zeros(material.shape, jnp.float32)
        for klass in range(disp_ref.shape[0]):
            here = material == klass
            kappa = jnp.where(here, disp_ref[klass], kappa)
            speed = jnp.where(here, perm_ref[klass], speed)
        kappa_ref[z] = kappa
        speed_ref[z] = speed
        return carry

    lax.fori_loop(0, depth, layer, 0)
    up_ref[2 * count] = kappa_ref[depth - 1]
    for t in range(count):
        flow = speed_ref[depth - 1] * tide_ref[t]
        up_ref[t] = last_ref[t, 0]
        up_ref[count + t] = jnp.where(flags_ref[t, 0, 0] != 0, -flow, flow)
        down_ref[t] = bottom_ref[t, 0]


def prep(disp_table, perm_table, tide, material, face_flags, field):
    count, _, depth, width, length = face_flags.shape
    smem = pl.BlockSpec(memory_space=pltpu.SMEM)
    cells = pl.BlockSpec((depth, width, length), lambda i: (0, 0, 0))
    up = (2 * count + 1, width, length)
    down = (count, width, length)
    return pl.pallas_call(
        prep_kernel,
        grid=(1,),
        in_specs=[
            smem,
            smem,
            smem,
            cells,
            pl.BlockSpec((count, 1, 1, width, length), lambda i: (0, 0, depth - 1, 0, 0)),
            pl.BlockSpec((count, 1, width, length), lambda i: (0, 0, 0, 0)),
            pl.BlockSpec((count, 1, width, length), lambda i: (0, depth - 1, 0, 0)),
        ],
        out_specs=[
            cells,
            cells,
            pl.BlockSpec(up, lambda i: (0, 0, 0)),
            pl.BlockSpec(down, lambda i: (0, 0, 0)),
        ],
        out_shape=[
            jax.ShapeDtypeStruct(material.shape, jnp.float32),
            jax.ShapeDtypeStruct(material.shape, jnp.float32),
            jax.ShapeDtypeStruct(up, jnp.float32),
            jax.ShapeDtypeStruct(down, jnp.float32),
        ],
        compiler_params=pltpu.CompilerParams(vmem_limit_bytes=VMEM),
        cost_estimate=COST,
        name="prep",
    )(disp_table, perm_table, tide, *in_hbm(material, face_flags, field, field))


def stencil_kernel(
    second, first, aliased, tide_ref, u_ref, low_ref, high_ref, flags_ref, src_ref, kappa_ref, speed_ref, below_k_ref, below_f_ref, *rest
):
    if second:
        winv_ref, out_ref = rest[0], rest[-1]
    else:
        out_ref, winv_ref = rest[aliased:]
    depth, width, length = u_ref.shape[1:]
    tide = tide_ref[first + pl.program_id(0)]
    row = lax.broadcasted_iota(jnp.int32, (width, length), 0)
    col = lax.broadcasted_iota(jnp.int32, (width, length), 1)
    last_row, last_col = row == width - 1, col == length - 1

    below_k, below_f = below_k_ref[0], below_f_ref[0]
    au_low = (below_k + jnp.maximum(below_f, 0.0)) * low_ref[0]
    b_low = below_k - jnp.minimum(below_f, 0.0)

    def layer(z, carry, u_up):
        au_low, b_low = carry
        u = u_ref[0, z]
        kappa = kappa_ref[z]
        full = kappa + speed_ref[z] * tide

        def coefs(dim):
            back = flags_ref[0, dim, z] != 0
            return jnp.where(back, kappa, full), jnp.where(back, full, kappa)

        a, b = coefs(0)
        total = b * u_up + au_low
        diag = (decay_rate + a) + b_low
        next_carry = (a * u, b)
        for dim, last in ((1, last_row), (2, last_col)):
            a, b = coefs(dim)
            size = u.shape[dim - 1]
            b = jnp.where(last, 0.0, b)
            au = jnp.where(last, 0.0, a * u)
            total = total + b * pltpu.roll(u, size - 1, dim - 1) + pltpu.roll(au, 1, dim - 1)
            if not second:
                diag = diag + (a + pltpu.roll(b, 1, dim - 1))
        if second:
            out_ref[0, z] = (1.0 - relax_weight) * u + winv_ref[0, z] * (total + src_ref[0, z])
        else:
            out_ref[0, z] = diag * u - total - src_ref[0, z]
            winv_ref[0, z] = relax_weight / diag
        return next_carry

    carry = lax.fori_loop(0, depth - 1, lambda z, c: layer(z, c, u_ref[0, z + 1]), (au_low, b_low))
    layer(depth - 1, carry, high_ref[0])


def stencil(second, part, tide, u, low, high, flags, src, kappa, speed, below, winv=None, before=()):
    count, depth, width, length = u.shape
    first, stop = count * part // PARTS, count * (part + 1) // PARTS
    field = pl.BlockSpec((1, depth, width, length), lambda t: (first + t, 0, 0, 0))
    plane = pl.BlockSpec((1, width, length), lambda t: (first + t, 0, 0))
    cells = pl.BlockSpec((depth, width, length), lambda t: (0, 0, 0))
    in_specs = [
        pl.BlockSpec(memory_space=pltpu.SMEM),
        field,
        plane,
        plane,
        pl.BlockSpec((1, 3, depth, width, length), lambda t: (first + t, 0, 0, 0, 0)),
        field,
        cells,
        cells,
        pl.BlockSpec((1, width, length), lambda t: (2 * count, 0, 0)),
        pl.BlockSpec((1, width, length), lambda t: (count + first + t, 0, 0)),
    ]
    args = [tide, *in_hbm(u), low, high, *in_hbm(flags, src), kappa, speed, below, below]
    if second:
        in_specs.append(field)
        args.extend(in_hbm(winv))
    aliases = {len(args) + i: i for i in range(len(before))}
    in_specs += [pl.BlockSpec(memory_space=pl.ANY)] * len(before)
    args.extend(in_hbm(*before))
    shape = pltpu.HBM(u.shape, jnp.float32)
    outs = 1 if second else 2
    return pl.pallas_call(
        functools.partial(stencil_kernel, second, first, len(before)),
        grid=(stop - first,),
        in_specs=in_specs,
        out_specs=[field] * outs,
        out_shape=[shape] * outs,
        input_output_aliases=aliases,
        compiler_params=pltpu.CompilerParams(vmem_limit_bytes=VMEM),
        cost_estimate=COST,
        name="stencil_two" if second else "stencil_one",
    )(*args)


def apply_kernel(n, me_ref, own_ref, *refs):
    received, mat_ref, outs = refs[: n - 1], refs[n - 1], refs[n:]
    parts = [own_ref, *received]
    count, _, width, length = own_ref.shape
    groups = width // SUB
    blocks = jnp.concatenate([part[:, 0] for part in parts], 0)
    wide = jnp.concatenate(
        [blocks[:, g * SUB : (g + 1) * SUB].reshape(NT * SUB, length) for g in range(groups)], 1
    )
    product = lax.dot_general(
        mat_ref[...],
        wide,
        (((1,), (0,)), ((), ())),
        precision=lax.Precision.HIGHEST,
        preferred_element_type=jnp.float32,
    )
    for g in range(groups):
        piece = product[:, g * length : (g + 1) * length].reshape(NT, SUB, length)
        for m, out in enumerate(outs):
            out[:, 0, g * SUB : (g + 1) * SUB] = piece[m * count : (m + 1) * count]


def apply_time(me, field, received, mat, chunk):
    n = len(received) + 1
    count, depth, width, length = field.shape
    part = received[0].shape[1]
    piece = pl.BlockSpec((count, 1, width, length), lambda i, me: (0, i, 0, 0))
    shape = jax.ShapeDtypeStruct(received[0].shape, jnp.float32)
    size = n * received[0].size
    return pl.pallas_call(
        functools.partial(apply_kernel, n),
        grid_spec=pltpu.PrefetchScalarGridSpec(
            num_scalar_prefetch=1,
            grid=(part,),
            in_specs=[
                pl.BlockSpec((count, 1, width, length), lambda i, me: (0, (chunk * n + me[0]) * part + i, 0, 0)),
                *([piece] * (n - 1)),
                pl.BlockSpec(mat.shape, lambda i, me: (0, 0)),
            ],
            out_specs=[piece] * n,
        ),
        out_shape=[shape] * n,
        compiler_params=pltpu.CompilerParams(vmem_limit_bytes=VMEM),
        cost_estimate=COST,
        name="apply_time",
    )(me, *in_hbm(field), *received, mat)


ROWS = 16


def first_kernel(n, aliased, me_ref, *refs):
    pieces, (s_ref, winv_ref, u_ref) = refs[:n], refs[n : n + 3]
    res_ref, mid_ref, first_ref, last_ref, *sends = refs[n + 3 + aliased :]
    part = pieces[0].shape[1]
    for m, piece in enumerate(pieces):
        for i in range(part):
            z = (me_ref[0] ^ m) * part + i
            res = s_ref[:, z] + piece[:, i]
            mid = u_ref[:, z] - winv_ref[:, z] * res
            res_ref[:, z] = res
            mid_ref[:, z] = mid
            if m:
                sends[m - 1][:, i] = mid
    first_ref[...] = mid_ref[:, 0]
    last_ref[...] = mid_ref[:, n * part - 1]


def first_update(me, pieces, s, winv, u, chunk, before):
    n = len(pieces)
    count, depth, width, length = u.shape
    part = pieces[0].shape[1]
    piece = pl.BlockSpec((count, part, ROWS, length), lambda i, me: (0, 0, i, 0))
    layers = pl.BlockSpec((count, n * part, ROWS, length), lambda i, me: (0, chunk, i, 0))
    whole = pltpu.HBM(u.shape, jnp.float32)
    aliased = len(before)
    size = n * pieces[0].size
    return pl.pallas_call(
        functools.partial(first_kernel, n, aliased),
        grid_spec=pltpu.PrefetchScalarGridSpec(
            num_scalar_prefetch=1,
            grid=(width // ROWS,),
            in_specs=[piece] * n + [layers] * 3 + [pl.BlockSpec(memory_space=pl.ANY)] * aliased,
            out_specs=[layers] * 2 + [pl.BlockSpec((count, ROWS, length), lambda i, me: (0, i, 0))] * 2 + [piece] * (n - 1),
        ),
        out_shape=[whole] * 2
        + [jax.ShapeDtypeStruct((count, width, length), jnp.float32)] * 2
        + [jax.ShapeDtypeStruct(pieces[0].shape, jnp.float32)] * (n - 1),
        input_output_aliases={n + 4 + i: i for i in range(aliased)},
        compiler_params=pltpu.CompilerParams(vmem_limit_bytes=VMEM),
        cost_estimate=COST,
        name="first_update",
    )(me, *pieces, *in_hbm(s, winv, u, *before))


def last_kernel(piece_ref, base_ref, winv_ref, *refs):
    refs[-1][...] = base_ref[...] - winv_ref[...] * piece_ref[...]


def last_update(me, piece, base, winv, n, chunk, m, before, held=None):
    count, part, width, length = piece.shape
    layers = pl.BlockSpec((count, part, width, length), lambda i, me: (0, chunk * n + (me[0] ^ m), 0, 0))
    block = pl.BlockSpec((count, part, width, length), lambda i, me: (0, 0, 0, 0))
    return pl.pallas_call(
        lambda me_ref, *refs: last_kernel(*refs),
        grid_spec=pltpu.PrefetchScalarGridSpec(
            num_scalar_prefetch=1,
            grid=(1,),
            in_specs=[block] + [block if held else layers] * 2 + [pl.BlockSpec(memory_space=pl.ANY)],
            out_specs=layers,
        ),
        out_shape=pltpu.HBM(base.shape, jnp.float32),
        input_output_aliases={4: 0},
        compiler_params=pltpu.CompilerParams(vmem_limit_bytes=VMEM),
        cost_estimate=COST,
        name="last_update",
    )(me, piece, *(held or in_hbm(base, winv)), *in_hbm(before))


def chunk_kernel(n, me_ref, *refs):
    pieces, (base_ref, winv_ref) = refs[:n], refs[n : n + 2]
    out_ref = refs[-1]
    part = pieces[0].shape[1]
    for m, piece in enumerate(pieces):
        for i in range(part):
            z = (me_ref[0] ^ m) * part + i
            out_ref[:, z] = base_ref[:, z] - winv_ref[:, z] * piece[:, i]


def chunk_update(me, pieces, base, winv, chunk, before):
    n = len(pieces)
    count, depth, width, length = base.shape
    part = pieces[0].shape[1]
    piece = pl.BlockSpec((count, part, ROWS, length), lambda i, me: (0, 0, i, 0))
    layers = pl.BlockSpec((count, n * part, ROWS, length), lambda i, me: (0, chunk, i, 0))
    return pl.pallas_call(
        functools.partial(chunk_kernel, n),
        grid_spec=pltpu.PrefetchScalarGridSpec(
            num_scalar_prefetch=1,
            grid=(width // ROWS,),
            in_specs=[piece] * n + [layers] * 2 + [pl.BlockSpec(memory_space=pl.ANY)] * len(before),
            out_specs=layers,
        ),
        out_shape=pltpu.HBM(base.shape, jnp.float32),
        input_output_aliases={n + 3: 0} if before else {},
        compiler_params=pltpu.CompilerParams(vmem_limit_bytes=VMEM),
        cost_estimate=COST,
        name="chunk_update",
    )(me, *pieces, *in_hbm(base, winv, *before))


def exchange(pieces):
    n = len(pieces) + 1
    return [
        lax.ppermute(piece, "inst", [(i, i ^ m) for i in range(n)]) for m, piece in enumerate(pieces, 1)
    ]


def after(arrays, *first):
    return lax.optimization_barrier((arrays, first))[0]


def upward(plane):
    return lax.ppermute(plane, "space", [(i, i + 1) for i in range(lax.axis_size("space") - 1)])


def downward(plane):
    return lax.ppermute(plane, "space", [(i + 1, i) for i in range(lax.axis_size("space") - 1)])


def body(field_start, source, material, face_flags, disp_table, perm_table):
    count, depth, width, length = field_start.shape
    n = lax.axis_size("inst")
    chunks = min(CHUNKS, depth // n)
    part = depth // (chunks * n)
    me = lax.axis_index("inst")
    me_array = me.reshape(1).astype(jnp.int32)

    far = cut(me_array, field_start, n, 0, part, [n - 1])
    near = cut(me_array, after(field_start, *far), n, 0, part, range(1, n - 1))
    going = near + far
    there = [exchange(going)]
    start, flags, material = after((field_start, face_flags, material), *going)

    moments = (me * count + jnp.arange(count)).astype(jnp.float32)
    tide = 1.0 + 0.5 * jnp.cos(2.0 * jnp.pi * moments / NT)
    mat = spectral_blocks(me, n, count)
    kappa, speed, up, down = prep(disp_table, perm_table, tide, material, flags, start)
    below, high = upward(up), downward(down)
    start = after(start, below, high)
    for chunk in range(1, chunks):
        going = cut(me_array, start, n, chunk, part)
        there.append(exchange(going))
        start = after(start, *going)
    shared = (below, high, flags, source, kappa, speed, below)
    first = stencil(False, 0, tide, start, *shared)

    back = []
    there[0] = after(there[0], first)
    for chunk in range(chunks):
        own, *rest = apply_time(me_array, field_start, there[chunk], mat, chunk)
        back.append([own] + exchange(rest))
    for half in range(1, PARTS):
        first = stencil(False, half, tide, after(field_start, back[0][1]), *shared, before=first)
    plain, winv = first

    whole = []
    there = []
    low = high = None
    for chunk in range(chunks):
        if chunk:
            back[chunk] = after(back[chunk], high)
        done = first_update(me_array, back[chunk], plain, winv, field_start, chunk, whole)
        whole, (bottom, last), sends = done[:2], done[2:4], done[4:]
        if chunk == 0:
            high = downward(bottom)
        if chunk == chunks - 1:
            low = upward(last)
        there.append(exchange(sends))
    residual, middle = whole
    there[0] = after(there[0], low)

    back = []
    second = ()
    for chunk in range(chunks):
        own, *rest = apply_time(me_array, middle, there[chunk], mat, chunk)
        back.append([own] + exchange(rest))
        if chunk < PARTS:
            ready = there[1][0] if chunk == 0 else back[0][1]
            now = after(middle, ready)
            second = stencil(True, chunk, tide, now, low, high, face_flags, source, kappa, speed, below, winv, second)
            if chunk == 0:
                there[1] = after(there[1], *second)
    base = second[0]

    field = []
    for chunk in range(chunks - 1):
        field = [chunk_update(me_array, back[chunk], base, winv, chunk, field)]
    chunk = chunks - 1
    held = [cut(me_array, array, n, chunk, part) for array in (base, winv)]
    for m, piece in enumerate(back[chunk]):
        there = [pieces[m - 1] for pieces in held] if m else None
        field = [last_update(me_array, piece, base, winv, n, chunk, m, field[0], there)]
        if m == 0:
            held, field = after((held, field), held)
    return (residual, field[0])


def solution(mesh):
    return jax.shard_map(
        body,
        mesh=mesh,
        in_specs=(
            P("inst", "space", None, None),
            P("inst", "space", None, None),
            P("space", None, None),
            P("inst", None, "space", None, None),
            P(),
            P(),
        ),
        out_specs=(P("inst", "space", None, None), P("inst", "space", None, None)),
        check_vma=False,
    )
```

```python
import functools

import jax
import jax.numpy as jnp
from jax import lax
from jax.experimental import pallas as pl
from jax.experimental.pallas import tpu as pltpu
from jax.sharding import PartitionSpec as P

NT = 32


omega_scale = 0.25
decay_rate = 0.3
relax_weight = 0.8

CHUNKS = 2
PARTS = 2
SUB = 8
VMEM = 20 << 20
COST = pl.CostEstimate(flops=1 << 10, bytes_accessed=1 << 10, transcendentals=0)


def code(m, n):
    return (n - m) % n


def spectral_blocks(me, n, count):
    spots = jnp.arange(NT)
    moments = (me ^ code(spots // count, n)) * count + spots % count
    diff = moments[:, None] - moments[None, :]
    angle = jnp.pi * diff.astype(jnp.float32) / NT
    parity = 1.0 - 2.0 * (diff % 2).astype(jnp.float32)
    safe = jnp.where(diff == 0, 1.0, jnp.sin(angle))
    dmat = omega_scale * jnp.where(diff == 0, 0.0, 0.5 * parity * jnp.cos(angle) / safe)
    rows = jnp.repeat(jnp.repeat(dmat, SUB, 0), SUB, 1)
    lane = jnp.arange(NT * SUB) % SUB
    return jnp.where(lane[:, None] == lane[None, :], rows, 0.0)


def in_hbm(*arrays):
    return [pltpu.with_memory_space_constraint(array, pltpu.HBM) for array in arrays]


def cut_kernel(me_ref, *refs):
    half = len(refs) // 2
    for source, out in zip(refs[:half], refs[half:]):
        out[...] = source[...]


def cut(me, field, n, chunk, part, partners=None):
    count, depth, width, length = field.shape
    partners = range(1, n) if partners is None else partners

    def block(m):
        return pl.BlockSpec(
            (count, part, width, length), lambda i, me: (0, chunk * n + (me[0] ^ code(m, n)), 0, 0)
        )

    piece = pl.BlockSpec((count, part, width, length), lambda i, me: (0, 0, 0, 0))
    return pl.pallas_call(
        cut_kernel,
        grid_spec=pltpu.PrefetchScalarGridSpec(
            num_scalar_prefetch=1,
            grid=(1,),
            in_specs=[block(m) for m in partners],
            out_specs=[piece] * len(partners),
        ),
        out_shape=[jax.ShapeDtypeStruct((count, part, width, length), jnp.float32)] * len(partners),
        compiler_params=pltpu.CompilerParams(vmem_limit_bytes=VMEM),
        cost_estimate=COST,
        name="cut",
    )(me, *in_hbm(*[field] * len(partners)))


def prep_kernel(
    disp_ref, perm_ref, tide_ref, material_ref, flags_ref, bottom_ref, last_ref, kappa_ref, speed_ref, up_ref, down_ref
):
    depth = material_ref.shape[0]
    count = flags_ref.shape[0]

    def layer(z, carry):
        material = material_ref[z]
        kappa = jnp.zeros(material.shape, jnp.float32)
        speed = jnp.zeros(material.shape, jnp.float32)
        for klass in range(disp_ref.shape[0]):
            here = material == klass
            kappa = jnp.where(here, disp_ref[klass], kappa)
            speed = jnp.where(here, perm_ref[klass], speed)
        kappa_ref[z] = kappa
        speed_ref[z] = speed
        return carry

    lax.fori_loop(0, depth, layer, 0)
    up_ref[2 * count] = kappa_ref[depth - 1]
    for t in range(count):
        flow = speed_ref[depth - 1] * tide_ref[t]
        up_ref[t] = last_ref[t, 0]
        up_ref[count + t] = jnp.where(flags_ref[t, 0, 0] != 0, -flow, flow)
        down_ref[t] = bottom_ref[t, 0]


def prep(disp_table, perm_table, tide, material, face_flags, field):
    count, _, depth, width, length = face_flags.shape
    smem = pl.BlockSpec(memory_space=pltpu.SMEM)
    cells = pl.BlockSpec((depth, width, length), lambda i: (0, 0, 0))
    up = (2 * count + 1, width, length)
    down = (count, width, length)
    return pl.pallas_call(
        prep_kernel,
        grid=(1,),
        in_specs=[
            smem,
            smem,
            smem,
            cells,
            pl.BlockSpec((count, 1, 1, width, length), lambda i: (0, 0, depth - 1, 0, 0)),
            pl.BlockSpec((count, 1, width, length), lambda i: (0, 0, 0, 0)),
            pl.BlockSpec((count, 1, width, length), lambda i: (0, depth - 1, 0, 0)),
        ],
        out_specs=[
            cells,
            cells,
            pl.BlockSpec(up, lambda i: (0, 0, 0)),
            pl.BlockSpec(down, lambda i: (0, 0, 0)),
        ],
        out_shape=[
            jax.ShapeDtypeStruct(material.shape, jnp.float32),
            jax.ShapeDtypeStruct(material.shape, jnp.float32),
            jax.ShapeDtypeStruct(up, jnp.float32),
            jax.ShapeDtypeStruct(down, jnp.float32),
        ],
        compiler_params=pltpu.CompilerParams(vmem_limit_bytes=VMEM),
        cost_estimate=COST,
        name="prep",
    )(disp_table, perm_table, tide, *in_hbm(material, face_flags, field, field))


def stencil_kernel(
    second, first, aliased, tide_ref, u_ref, low_ref, high_ref, flags_ref, src_ref, kappa_ref, speed_ref, below_k_ref, below_f_ref, *rest
):
    if second:
        winv_ref, out_ref = rest[0], rest[-1]
    else:
        out_ref, winv_ref = rest[aliased:]
    depth, width, length = u_ref.shape[1:]
    tide = tide_ref[first + pl.program_id(0)]
    row = lax.broadcasted_iota(jnp.int32, (width, length), 0)
    col = lax.broadcasted_iota(jnp.int32, (width, length), 1)
    last_row, last_col = row == width - 1, col == length - 1

    below_k, below_f = below_k_ref[0], below_f_ref[0]
    au_low = (below_k + jnp.maximum(below_f, 0.0)) * low_ref[0]
    b_low = below_k - jnp.minimum(below_f, 0.0)

    def layer(z, carry, u_up):
        au_low, b_low = carry
        u = u_ref[0, z]
        kappa = kappa_ref[z]
        full = kappa + speed_ref[z] * tide

        def coefs(dim):
            back = flags_ref[0, dim, z] != 0
            return jnp.where(back, kappa, full), jnp.where(back, full, kappa)

        a, b = coefs(0)
        total = b * u_up + au_low
        diag = (decay_rate + a) + b_low
        next_carry = (a * u, b)
        for dim, last in ((1, last_row), (2, last_col)):
            a, b = coefs(dim)
            size = u.shape[dim - 1]
            b = jnp.where(last, 0.0, b)
            au = jnp.where(last, 0.0, a * u)
            total = total + b * pltpu.roll(u, size - 1, dim - 1) + pltpu.roll(au, 1, dim - 1)
            if not second:
                diag = diag + (a + pltpu.roll(b, 1, dim - 1))
        if second:
            out_ref[0, z] = (1.0 - relax_weight) * u + winv_ref[0, z] * (total + src_ref[0, z])
        else:
            out_ref[0, z] = diag * u - total - src_ref[0, z]
            winv_ref[0, z] = relax_weight / diag
        return next_carry

    carry = lax.fori_loop(0, depth - 1, lambda z, c: layer(z, c, u_ref[0, z + 1]), (au_low, b_low))
    layer(depth - 1, carry, high_ref[0])


def stencil(second, part, tide, u, low, high, flags, src, kappa, speed, below, winv=None, before=()):
    count, depth, width, length = u.shape
    first, stop = count * part // PARTS, count * (part + 1) // PARTS
    field = pl.BlockSpec((1, depth, width, length), lambda t: (first + t, 0, 0, 0))
    plane = pl.BlockSpec((1, width, length), lambda t: (first + t, 0, 0))
    cells = pl.BlockSpec((depth, width, length), lambda t: (0, 0, 0))
    in_specs = [
        pl.BlockSpec(memory_space=pltpu.SMEM),
        field,
        plane,
        plane,
        pl.BlockSpec((1, 3, depth, width, length), lambda t: (first + t, 0, 0, 0, 0)),
        field,
        cells,
        cells,
        pl.BlockSpec((1, width, length), lambda t: (2 * count, 0, 0)),
        pl.BlockSpec((1, width, length), lambda t: (count + first + t, 0, 0)),
    ]
    args = [tide, *in_hbm(u), low, high, *in_hbm(flags, src), kappa, speed, below, below]
    if second:
        in_specs.append(field)
        args.extend(in_hbm(winv))
    aliases = {len(args) + i: i for i in range(len(before))}
    in_specs += [pl.BlockSpec(memory_space=pl.ANY)] * len(before)
    args.extend(in_hbm(*before))
    shape = pltpu.HBM(u.shape, jnp.float32)
    outs = 1 if second else 2
    return pl.pallas_call(
        functools.partial(stencil_kernel, second, first, len(before)),
        grid=(stop - first,),
        in_specs=in_specs,
        out_specs=[field] * outs,
        out_shape=[shape] * outs,
        input_output_aliases=aliases,
        compiler_params=pltpu.CompilerParams(vmem_limit_bytes=VMEM),
        cost_estimate=COST,
        name="stencil_two" if second else "stencil_one",
    )(*args)


def apply_kernel(n, me_ref, own_ref, *refs):
    received, mat_ref, outs = refs[: n - 1], refs[n - 1], refs[n:]
    parts = [own_ref, *received]
    count, _, width, length = own_ref.shape
    groups = width // SUB
    blocks = jnp.concatenate([part[:, 0] for part in parts], 0)
    wide = jnp.concatenate(
        [blocks[:, g * SUB : (g + 1) * SUB].reshape(NT * SUB, length) for g in range(groups)], 1
    )
    product = lax.dot_general(
        mat_ref[...],
        wide,
        (((1,), (0,)), ((), ())),
        precision=lax.Precision.HIGHEST,
        preferred_element_type=jnp.float32,
    )
    for g in range(groups):
        piece = product[:, g * length : (g + 1) * length].reshape(NT, SUB, length)
        for m, out in enumerate(outs):
            out[:, 0, g * SUB : (g + 1) * SUB] = piece[m * count : (m + 1) * count]


def apply_time(me, field, received, mat, chunk):
    n = len(received) + 1
    count, depth, width, length = field.shape
    part = received[0].shape[1]
    piece = pl.BlockSpec((count, 1, width, length), lambda i, me: (0, i, 0, 0))
    shape = jax.ShapeDtypeStruct(received[0].shape, jnp.float32)
    size = n * received[0].size
    return pl.pallas_call(
        functools.partial(apply_kernel, n),
        grid_spec=pltpu.PrefetchScalarGridSpec(
            num_scalar_prefetch=1,
            grid=(part,),
            in_specs=[
                pl.BlockSpec((count, 1, width, length), lambda i, me: (0, (chunk * n + me[0]) * part + i, 0, 0)),
                *([piece] * (n - 1)),
                pl.BlockSpec(mat.shape, lambda i, me: (0, 0)),
            ],
            out_specs=[piece] * n,
        ),
        out_shape=[shape] * n,
        compiler_params=pltpu.CompilerParams(vmem_limit_bytes=VMEM),
        cost_estimate=COST,
        name="apply_time",
    )(me, *in_hbm(field), *received, mat)


ROWS = 16


def first_kernel(n, aliased, me_ref, *refs):
    pieces, (s_ref, winv_ref, u_ref) = refs[:n], refs[n : n + 3]
    res_ref, mid_ref, first_ref, last_ref, *sends = refs[n + 3 + aliased :]
    part = pieces[0].shape[1]
    for m, piece in enumerate(pieces):
        for i in range(part):
            z = (me_ref[0] ^ code(m, n)) * part + i
            res = s_ref[:, z] + piece[:, i]
            mid = u_ref[:, z] - winv_ref[:, z] * res
            res_ref[:, z] = res
            mid_ref[:, z] = mid
            if m:
                sends[m - 1][:, i] = mid
    first_ref[...] = mid_ref[:, 0]
    last_ref[...] = mid_ref[:, n * part - 1]


def first_update(me, pieces, s, winv, u, chunk, before):
    n = len(pieces)
    count, depth, width, length = u.shape
    part = pieces[0].shape[1]
    piece = pl.BlockSpec((count, part, ROWS, length), lambda i, me: (0, 0, i, 0))
    layers = pl.BlockSpec((count, n * part, ROWS, length), lambda i, me: (0, chunk, i, 0))
    whole = pltpu.HBM(u.shape, jnp.float32)
    aliased = len(before)
    size = n * pieces[0].size
    return pl.pallas_call(
        functools.partial(first_kernel, n, aliased),
        grid_spec=pltpu.PrefetchScalarGridSpec(
            num_scalar_prefetch=1,
            grid=(width // ROWS,),
            in_specs=[piece] * n + [layers] * 3 + [pl.BlockSpec(memory_space=pl.ANY)] * aliased,
            out_specs=[layers] * 2 + [pl.BlockSpec((count, ROWS, length), lambda i, me: (0, i, 0))] * 2 + [piece] * (n - 1),
        ),
        out_shape=[whole] * 2
        + [jax.ShapeDtypeStruct((count, width, length), jnp.float32)] * 2
        + [jax.ShapeDtypeStruct(pieces[0].shape, jnp.float32)] * (n - 1),
        input_output_aliases={n + 4 + i: i for i in range(aliased)},
        compiler_params=pltpu.CompilerParams(vmem_limit_bytes=VMEM),
        cost_estimate=COST,
        name="first_update",
    )(me, *pieces, *in_hbm(s, winv, u, *before))


def last_kernel(piece_ref, base_ref, winv_ref, *refs):
    refs[-1][...] = base_ref[...] - winv_ref[...] * piece_ref[...]


def last_update(me, piece, base, winv, n, chunk, m, before, held=None):
    count, part, width, length = piece.shape
    layers = pl.BlockSpec((count, part, width, length), lambda i, me: (0, chunk * n + (me[0] ^ code(m, n)), 0, 0))
    block = pl.BlockSpec((count, part, width, length), lambda i, me: (0, 0, 0, 0))
    return pl.pallas_call(
        lambda me_ref, *refs: last_kernel(*refs),
        grid_spec=pltpu.PrefetchScalarGridSpec(
            num_scalar_prefetch=1,
            grid=(1,),
            in_specs=[block] + [block if held else layers] * 2 + [pl.BlockSpec(memory_space=pl.ANY)],
            out_specs=layers,
        ),
        out_shape=pltpu.HBM(base.shape, jnp.float32),
        input_output_aliases={4: 0},
        compiler_params=pltpu.CompilerParams(vmem_limit_bytes=VMEM),
        cost_estimate=COST,
        name="last_update",
    )(me, piece, *(held or in_hbm(base, winv)), *in_hbm(before))


def final_kernel(n, spots, me_ref, *refs):
    count = len(spots)
    pieces, bases, winvs = refs[:count], refs[count : 2 * count], refs[2 * count : 3 * count]
    out_ref, sums, sems = refs[3 * count + 1 :]
    part = pieces[0].shape[1]
    copies = []
    for p, (first, m) in enumerate(spots):
        for i in range(part):
            sums[p, :, i] = bases[p][:, i] - winvs[p][:, i] * pieces[p][:, i]
            place = (first + (me_ref[0] ^ code(m, n))) * part + i
            copy = pltpu.make_async_copy(
                sums.at[p, :, pl.ds(i, 1)], out_ref.at[:, pl.ds(place, 1)], sems.at[p, i]
            )
            copy.start()
            copies.append(copy)
    for copy in copies:
        copy.wait()


def final_update(me, pieces, bases, winvs, n, spots, before):
    vmem = pl.BlockSpec(memory_space=pltpu.VMEM)
    anywhere = pl.BlockSpec(memory_space=pl.ANY)
    count = len(pieces)
    return pl.pallas_call(
        functools.partial(final_kernel, n, spots),
        in_specs=[pl.BlockSpec(memory_space=pltpu.SMEM)] + [vmem] * (3 * count) + [anywhere],
        out_specs=anywhere,
        out_shape=pltpu.HBM(before.shape, jnp.float32),
        scratch_shapes=[
            pltpu.VMEM((count, *pieces[0].shape), jnp.float32),
            pltpu.SemaphoreType.DMA((count, pieces[0].shape[1])),
        ],
        input_output_aliases={3 * count + 1: 0},
        compiler_params=pltpu.CompilerParams(vmem_limit_bytes=VMEM),
        cost_estimate=COST,
        name="final_update",
    )(me, *pieces, *bases, *winvs, *in_hbm(before))


def chunk_kernel(n, me_ref, *refs):
    pieces, (base_ref, winv_ref) = refs[:n], refs[n : n + 2]
    out_ref = refs[-1]
    part = pieces[0].shape[1]
    for m, piece in enumerate(pieces):
        for i in range(part):
            z = (me_ref[0] ^ code(m, n)) * part + i
            out_ref[:, z] = base_ref[:, z] - winv_ref[:, z] * piece[:, i]


def chunk_update(me, pieces, base, winv, chunk, before):
    n = len(pieces)
    count, depth, width, length = base.shape
    part = pieces[0].shape[1]
    piece = pl.BlockSpec((count, part, ROWS, length), lambda i, me: (0, 0, i, 0))
    layers = pl.BlockSpec((count, n * part, ROWS, length), lambda i, me: (0, chunk, i, 0))
    return pl.pallas_call(
        functools.partial(chunk_kernel, n),
        grid_spec=pltpu.PrefetchScalarGridSpec(
            num_scalar_prefetch=1,
            grid=(width // ROWS,),
            in_specs=[piece] * n + [layers] * 2 + [pl.BlockSpec(memory_space=pl.ANY)] * len(before),
            out_specs=layers,
        ),
        out_shape=pltpu.HBM(base.shape, jnp.float32),
        input_output_aliases={n + 3: 0} if before else {},
        compiler_params=pltpu.CompilerParams(vmem_limit_bytes=VMEM),
        cost_estimate=COST,
        name="chunk_update",
    )(me, *pieces, *in_hbm(base, winv, *before))


def exchange(pieces):
    n = len(pieces) + 1
    return [
        lax.ppermute(piece, "inst", [(i, i ^ code(m, n)) for i in range(n)]) for m, piece in enumerate(pieces, 1)
    ]


def after(arrays, *first):
    return lax.optimization_barrier((arrays, first))[0]


def upward(plane):
    return lax.ppermute(plane, "space", [(i, i + 1) for i in range(lax.axis_size("space") - 1)])


def downward(plane):
    return lax.ppermute(plane, "space", [(i + 1, i) for i in range(lax.axis_size("space") - 1)])


def body(field_start, source, material, face_flags, disp_table, perm_table):
    count, depth, width, length = field_start.shape
    n = lax.axis_size("inst")
    chunks = min(CHUNKS, depth // n)
    part = depth // (chunks * n)
    me = lax.axis_index("inst")
    me_array = me.reshape(1).astype(jnp.int32)

    far = cut(me_array, field_start, n, 0, part, [1])
    near = cut(me_array, after(field_start, *far), n, 0, part, range(2, n))
    going = far + near
    there = [exchange(going)]
    start, flags, material = after((field_start, face_flags, material), *going)

    moments = (me * count + jnp.arange(count)).astype(jnp.float32)
    tide = 1.0 + 0.5 * jnp.cos(2.0 * jnp.pi * moments / NT)
    mat = spectral_blocks(me, n, count)
    kappa, speed, up, down = prep(disp_table, perm_table, tide, material, flags, start)
    below, high = upward(up), downward(down)
    start = after(start, below, high)
    for chunk in range(1, chunks):
        going = cut(me_array, start, n, chunk, part)
        there.append(exchange(going))
        start = after(start, *going)
    shared = (below, high, flags, source, kappa, speed, below)
    first = stencil(False, 0, tide, start, *shared)

    back = []
    there[0] = after(there[0], first)
    for chunk in range(chunks):
        own, *rest = apply_time(me_array, field_start, there[chunk], mat, chunk)
        back.append([own] + exchange(rest))
    for half in range(1, PARTS):
        first = stencil(False, half, tide, after(field_start, back[0][1]), *shared, before=first)
    plain, winv = first

    whole = []
    there = []
    low = high = None
    for chunk in range(chunks):
        if chunk:
            back[chunk] = after(back[chunk], high)
        done = first_update(me_array, back[chunk], plain, winv, field_start, chunk, whole)
        whole, (bottom, last), sends = done[:2], done[2:4], done[4:]
        if chunk == 0:
            high = downward(bottom)
        if chunk == chunks - 1:
            low = upward(last)
        there.append(exchange(sends))
    residual, middle = whole
    there[0] = after(there[0], low)

    back = []
    second = ()
    for chunk in range(chunks):
        own, *rest = apply_time(me_array, middle, there[chunk], mat, chunk)
        back.append([own] + exchange(rest))
        if chunk < PARTS:
            ready = there[1][0] if chunk == 0 else back[0][1]
            now = after(middle, ready)
            second = stencil(True, chunk, tide, now, low, high, face_flags, source, kappa, speed, below, winv, second)
            if chunk == 0:
                there[1] = after(there[1], *second)
    base = second[0]

    field = []
    for chunk in range(chunks - 1):
        field = [chunk_update(me_array, back[chunk], base, winv, chunk, field)]
    chunk = chunks - 1
    held = [cut(me_array, array, n, chunk, part) for array in (base, winv)]
    late = max(1, n - 2)
    for m, piece in enumerate(back[chunk][:late]):
        there = [pieces[m - 1] for pieces in held] if m else None
        field = [last_update(me_array, piece, base, winv, n, chunk, m, field[0], there)]
        if m == 0:
            held, field = after((held, field), held)
    bases, winvs = (pieces[late - 1 :] for pieces in held)
    spots = [(chunk * n, m) for m in range(late, n)]
    return (residual, final_update(me_array, back[chunk][late:], bases, winvs, n, spots, field[0]))


def solution(mesh):
    return jax.shard_map(
        body,
        mesh=mesh,
        in_specs=(
            P("inst", "space", None, None),
            P("inst", "space", None, None),
            P("space", None, None),
            P("inst", None, "space", None, None),
            P(),
            P(),
        ),
        out_specs=(P("inst", "space", None, None), P("inst", "space", None, None)),
        check_vma=False,
    )
```

```python
import functools

import jax
import jax.numpy as jnp
from jax import lax
from jax.experimental import pallas as pl
from jax.experimental.pallas import tpu as pltpu
from jax.sharding import PartitionSpec as P

NT = 32


omega_scale = 0.25
decay_rate = 0.3
relax_weight = 0.8

CHUNKS = 2
PARTS = 2
SUB = 8
VMEM = 20 << 20
COST = pl.CostEstimate(flops=1 << 10, bytes_accessed=1 << 10, transcendentals=0)


def code(m, n):
    return (n - m) % n


def spectral_blocks(me, n, count):
    spots = jnp.arange(NT)
    moments = (me ^ code(spots // count, n)) * count + spots % count
    diff = moments[:, None] - moments[None, :]
    angle = jnp.pi * diff.astype(jnp.float32) / NT
    parity = 1.0 - 2.0 * (diff % 2).astype(jnp.float32)
    safe = jnp.where(diff == 0, 1.0, jnp.sin(angle))
    dmat = omega_scale * jnp.where(diff == 0, 0.0, 0.5 * parity * jnp.cos(angle) / safe)
    rows = jnp.repeat(jnp.repeat(dmat, SUB, 0), SUB, 1)
    lane = jnp.arange(NT * SUB) % SUB
    return jnp.where(lane[:, None] == lane[None, :], rows, 0.0)


def in_hbm(*arrays):
    return [pltpu.with_memory_space_constraint(array, pltpu.HBM) for array in arrays]


def cut_kernel(me_ref, *refs):
    half = len(refs) // 2
    for source, out in zip(refs[:half], refs[half:]):
        out[...] = source[...]


def cut(me, field, n, chunk, part, partners=None):
    count, depth, width, length = field.shape
    partners = range(1, n) if partners is None else partners

    def block(m):
        return pl.BlockSpec(
            (count, part, width, length), lambda i, me: (0, chunk * n + (me[0] ^ code(m, n)), 0, 0)
        )

    piece = pl.BlockSpec((count, part, width, length), lambda i, me: (0, 0, 0, 0))
    return pl.pallas_call(
        cut_kernel,
        grid_spec=pltpu.PrefetchScalarGridSpec(
            num_scalar_prefetch=1,
            grid=(1,),
            in_specs=[block(m) for m in partners],
            out_specs=[piece] * len(partners),
        ),
        out_shape=[jax.ShapeDtypeStruct((count, part, width, length), jnp.float32)] * len(partners),
        compiler_params=pltpu.CompilerParams(vmem_limit_bytes=VMEM),
        cost_estimate=COST,
        name="cut",
    )(me, *in_hbm(*[field] * len(partners)))


def prep_kernel(
    disp_ref, perm_ref, tide_ref, material_ref, flags_ref, bottom_ref, last_ref, kappa_ref, speed_ref, up_ref, down_ref
):
    depth = material_ref.shape[0]
    count = flags_ref.shape[0]

    def layer(z, carry):
        material = material_ref[z]
        kappa = jnp.zeros(material.shape, jnp.float32)
        speed = jnp.zeros(material.shape, jnp.float32)
        for klass in range(disp_ref.shape[0]):
            here = material == klass
            kappa = jnp.where(here, disp_ref[klass], kappa)
            speed = jnp.where(here, perm_ref[klass], speed)
        kappa_ref[z] = kappa
        speed_ref[z] = speed
        return carry

    lax.fori_loop(0, depth, layer, 0)
    up_ref[2 * count] = kappa_ref[depth - 1]
    for t in range(count):
        flow = speed_ref[depth - 1] * tide_ref[t]
        up_ref[t] = last_ref[t, 0]
        up_ref[count + t] = jnp.where(flags_ref[t, 0, 0] != 0, -flow, flow)
        down_ref[t] = bottom_ref[t, 0]


def prep(disp_table, perm_table, tide, material, face_flags, field):
    count, _, depth, width, length = face_flags.shape
    smem = pl.BlockSpec(memory_space=pltpu.SMEM)
    cells = pl.BlockSpec((depth, width, length), lambda i: (0, 0, 0))
    up = (2 * count + 1, width, length)
    down = (count, width, length)
    return pl.pallas_call(
        prep_kernel,
        grid=(1,),
        in_specs=[
            smem,
            smem,
            smem,
            cells,
            pl.BlockSpec((count, 1, 1, width, length), lambda i: (0, 0, depth - 1, 0, 0)),
            pl.BlockSpec((count, 1, width, length), lambda i: (0, 0, 0, 0)),
            pl.BlockSpec((count, 1, width, length), lambda i: (0, depth - 1, 0, 0)),
        ],
        out_specs=[
            cells,
            cells,
            pl.BlockSpec(up, lambda i: (0, 0, 0)),
            pl.BlockSpec(down, lambda i: (0, 0, 0)),
        ],
        out_shape=[
            jax.ShapeDtypeStruct(material.shape, jnp.float32),
            jax.ShapeDtypeStruct(material.shape, jnp.float32),
            jax.ShapeDtypeStruct(up, jnp.float32),
            jax.ShapeDtypeStruct(down, jnp.float32),
        ],
        compiler_params=pltpu.CompilerParams(vmem_limit_bytes=VMEM),
        cost_estimate=COST,
        name="prep",
    )(disp_table, perm_table, tide, *in_hbm(material, face_flags, field, field))


def stencil_kernel(
    second, first, aliased, tide_ref, u_ref, low_ref, high_ref, flags_ref, src_ref, kappa_ref, speed_ref, below_k_ref, below_f_ref, *rest
):
    if second:
        winv_ref, out_ref = rest[0], rest[-1]
    else:
        out_ref, winv_ref = rest[aliased:]
    depth, width, length = u_ref.shape[1:]
    tide = tide_ref[first + pl.program_id(0)]
    row = lax.broadcasted_iota(jnp.int32, (width, length), 0)
    col = lax.broadcasted_iota(jnp.int32, (width, length), 1)
    last_row, last_col = row == width - 1, col == length - 1

    below_k, below_f = below_k_ref[0], below_f_ref[0]
    au_low = (below_k + jnp.maximum(below_f, 0.0)) * low_ref[0]
    b_low = below_k - jnp.minimum(below_f, 0.0)

    def layer(z, carry, u_up):
        au_low, b_low = carry
        u = u_ref[0, z]
        kappa = kappa_ref[z]
        full = kappa + speed_ref[z] * tide

        def coefs(dim):
            back = flags_ref[0, dim, z] != 0
            return jnp.where(back, kappa, full), jnp.where(back, full, kappa)

        a, b = coefs(0)
        total = b * u_up + au_low
        diag = (decay_rate + a) + b_low
        next_carry = (a * u, b)
        for dim, last in ((1, last_row), (2, last_col)):
            a, b = coefs(dim)
            size = u.shape[dim - 1]
            b = jnp.where(last, 0.0, b)
            au = jnp.where(last, 0.0, a * u)
            total = total + b * pltpu.roll(u, size - 1, dim - 1) + pltpu.roll(au, 1, dim - 1)
            if not second:
                diag = diag + (a + pltpu.roll(b, 1, dim - 1))
        if second:
            out_ref[0, z] = (1.0 - relax_weight) * u + winv_ref[0, z] * (total + src_ref[0, z])
        else:
            out_ref[0, z] = diag * u - total - src_ref[0, z]
            winv_ref[0, z] = relax_weight / diag
        return next_carry

    carry = lax.fori_loop(0, depth - 1, lambda z, c: layer(z, c, u_ref[0, z + 1]), (au_low, b_low))
    layer(depth - 1, carry, high_ref[0])


def stencil(second, part, tide, u, low, high, flags, src, kappa, speed, below, winv=None, before=()):
    count, depth, width, length = u.shape
    first, stop = count * part // PARTS, count * (part + 1) // PARTS
    field = pl.BlockSpec((1, depth, width, length), lambda t: (first + t, 0, 0, 0))
    plane = pl.BlockSpec((1, width, length), lambda t: (first + t, 0, 0))
    cells = pl.BlockSpec((depth, width, length), lambda t: (0, 0, 0))
    in_specs = [
        pl.BlockSpec(memory_space=pltpu.SMEM),
        field,
        plane,
        plane,
        pl.BlockSpec((1, 3, depth, width, length), lambda t: (first + t, 0, 0, 0, 0)),
        field,
        cells,
        cells,
        pl.BlockSpec((1, width, length), lambda t: (2 * count, 0, 0)),
        pl.BlockSpec((1, width, length), lambda t: (count + first + t, 0, 0)),
    ]
    args = [tide, *in_hbm(u), low, high, *in_hbm(flags, src), kappa, speed, below, below]
    if second:
        in_specs.append(field)
        args.extend(in_hbm(winv))
    aliases = {len(args) + i: i for i in range(len(before))}
    in_specs += [pl.BlockSpec(memory_space=pl.ANY)] * len(before)
    args.extend(in_hbm(*before))
    shape = pltpu.HBM(u.shape, jnp.float32)
    outs = 1 if second else 2
    return pl.pallas_call(
        functools.partial(stencil_kernel, second, first, len(before)),
        grid=(stop - first,),
        in_specs=in_specs,
        out_specs=[field] * outs,
        out_shape=[shape] * outs,
        input_output_aliases=aliases,
        compiler_params=pltpu.CompilerParams(vmem_limit_bytes=VMEM),
        cost_estimate=COST,
        name="stencil_two" if second else "stencil_one",
    )(*args)


def apply_kernel(n, me_ref, own_ref, *refs):
    received, mat_ref, outs = refs[: n - 1], refs[n - 1], refs[n:]
    parts = [own_ref, *received]
    count, _, width, length = own_ref.shape
    groups = width // SUB
    blocks = jnp.concatenate([part[:, 0] for part in parts], 0)
    wide = jnp.concatenate(
        [blocks[:, g * SUB : (g + 1) * SUB].reshape(NT * SUB, length) for g in range(groups)], 1
    )
    product = lax.dot_general(
        mat_ref[...],
        wide,
        (((1,), (0,)), ((), ())),
        precision=lax.Precision.HIGHEST,
        preferred_element_type=jnp.float32,
    )
    for g in range(groups):
        piece = product[:, g * length : (g + 1) * length].reshape(NT, SUB, length)
        for m, out in enumerate(outs):
            out[:, 0, g * SUB : (g + 1) * SUB] = piece[m * count : (m + 1) * count]


def apply_time(me, field, received, mat, chunk):
    n = len(received) + 1
    count, depth, width, length = field.shape
    part = received[0].shape[1]
    piece = pl.BlockSpec((count, 1, width, length), lambda i, me: (0, i, 0, 0))
    shape = jax.ShapeDtypeStruct(received[0].shape, jnp.float32)
    size = n * received[0].size
    return pl.pallas_call(
        functools.partial(apply_kernel, n),
        grid_spec=pltpu.PrefetchScalarGridSpec(
            num_scalar_prefetch=1,
            grid=(part,),
            in_specs=[
                pl.BlockSpec((count, 1, width, length), lambda i, me: (0, (chunk * n + me[0]) * part + i, 0, 0)),
                *([piece] * (n - 1)),
                pl.BlockSpec(mat.shape, lambda i, me: (0, 0)),
            ],
            out_specs=[piece] * n,
        ),
        out_shape=[shape] * n,
        compiler_params=pltpu.CompilerParams(vmem_limit_bytes=VMEM),
        cost_estimate=COST,
        name="apply_time",
    )(me, *in_hbm(field), *received, mat)


ROWS = 16


def first_kernel(n, aliased, me_ref, *refs):
    pieces, (s_ref, winv_ref, u_ref) = refs[:n], refs[n : n + 3]
    res_ref, mid_ref, first_ref, last_ref, *sends = refs[n + 3 + aliased :]
    part = pieces[0].shape[1]
    for m, piece in enumerate(pieces):
        for i in range(part):
            z = (me_ref[0] ^ code(m, n)) * part + i
            res = s_ref[:, z] + piece[:, i]
            mid = u_ref[:, z] - winv_ref[:, z] * res
            res_ref[:, z] = res
            mid_ref[:, z] = mid
            if m:
                sends[m - 1][:, i] = mid
    first_ref[...] = mid_ref[:, 0]
    last_ref[...] = mid_ref[:, n * part - 1]


def first_update(me, pieces, s, winv, u, chunk, before):
    n = len(pieces)
    count, depth, width, length = u.shape
    part = pieces[0].shape[1]
    piece = pl.BlockSpec((count, part, ROWS, length), lambda i, me: (0, 0, i, 0))
    layers = pl.BlockSpec((count, n * part, ROWS, length), lambda i, me: (0, chunk, i, 0))
    whole = pltpu.HBM(u.shape, jnp.float32)
    aliased = len(before)
    size = n * pieces[0].size
    return pl.pallas_call(
        functools.partial(first_kernel, n, aliased),
        grid_spec=pltpu.PrefetchScalarGridSpec(
            num_scalar_prefetch=1,
            grid=(width // ROWS,),
            in_specs=[piece] * n + [layers] * 3 + [pl.BlockSpec(memory_space=pl.ANY)] * aliased,
            out_specs=[layers] * 2 + [pl.BlockSpec((count, ROWS, length), lambda i, me: (0, i, 0))] * 2 + [piece] * (n - 1),
        ),
        out_shape=[whole] * 2
        + [jax.ShapeDtypeStruct((count, width, length), jnp.float32)] * 2
        + [jax.ShapeDtypeStruct(pieces[0].shape, jnp.float32)] * (n - 1),
        input_output_aliases={n + 4 + i: i for i in range(aliased)},
        compiler_params=pltpu.CompilerParams(vmem_limit_bytes=VMEM),
        cost_estimate=COST,
        name="first_update",
    )(me, *pieces, *in_hbm(s, winv, u, *before))


def last_kernel(piece_ref, base_ref, winv_ref, *refs):
    refs[-1][...] = base_ref[...] - winv_ref[...] * piece_ref[...]


def last_update(me, piece, base, winv, n, chunk, m, before, held=None):
    count, part, width, length = piece.shape
    layers = pl.BlockSpec((count, part, width, length), lambda i, me: (0, chunk * n + (me[0] ^ code(m, n)), 0, 0))
    block = pl.BlockSpec((count, part, width, length), lambda i, me: (0, 0, 0, 0))
    return pl.pallas_call(
        lambda me_ref, *refs: last_kernel(*refs),
        grid_spec=pltpu.PrefetchScalarGridSpec(
            num_scalar_prefetch=1,
            grid=(1,),
            in_specs=[block] + [block if held else layers] * 2 + [pl.BlockSpec(memory_space=pl.ANY)],
            out_specs=layers,
        ),
        out_shape=pltpu.HBM(base.shape, jnp.float32),
        input_output_aliases={4: 0},
        compiler_params=pltpu.CompilerParams(vmem_limit_bytes=VMEM),
        cost_estimate=COST,
        name="last_update",
    )(me, piece, *(held or in_hbm(base, winv)), *in_hbm(before))


def final_kernel(n, spots, me_ref, *refs):
    count = len(spots)
    pieces, bases, winvs = refs[:count], refs[count : 2 * count], refs[2 * count : 3 * count]
    out_ref, sums, sems = refs[3 * count + 1 :]
    part = pieces[0].shape[1]
    copies = []
    for p, (first, m) in enumerate(spots):
        for i in range(part):
            sums[p, :, i] = bases[p][:, i] - winvs[p][:, i] * pieces[p][:, i]
            place = (first + (me_ref[0] ^ code(m, n))) * part + i
            copy = pltpu.make_async_copy(
                sums.at[p, :, pl.ds(i, 1)], out_ref.at[:, pl.ds(place, 1)], sems.at[p, i]
            )
            copy.start()
            copies.append(copy)
    for copy in copies:
        copy.wait()


def final_update(me, pieces, bases, winvs, n, spots, before):
    vmem = pl.BlockSpec(memory_space=pltpu.VMEM)
    anywhere = pl.BlockSpec(memory_space=pl.ANY)
    count = len(pieces)
    return pl.pallas_call(
        functools.partial(final_kernel, n, spots),
        in_specs=[pl.BlockSpec(memory_space=pltpu.SMEM)] + [vmem] * (3 * count) + [anywhere],
        out_specs=anywhere,
        out_shape=pltpu.HBM(before.shape, jnp.float32),
        scratch_shapes=[
            pltpu.VMEM((count, *pieces[0].shape), jnp.float32),
            pltpu.SemaphoreType.DMA((count, pieces[0].shape[1])),
        ],
        input_output_aliases={3 * count + 1: 0},
        compiler_params=pltpu.CompilerParams(vmem_limit_bytes=VMEM),
        cost_estimate=COST,
        name="final_update",
    )(me, *pieces, *bases, *winvs, *in_hbm(before))


def chunk_kernel(n, me_ref, *refs):
    pieces, (base_ref, winv_ref) = refs[:n], refs[n : n + 2]
    out_ref = refs[-1]
    part = pieces[0].shape[1]
    for m, piece in enumerate(pieces):
        for i in range(part):
            z = (me_ref[0] ^ code(m, n)) * part + i
            out_ref[:, z] = base_ref[:, z] - winv_ref[:, z] * piece[:, i]


def chunk_update(me, pieces, base, winv, chunk, before):
    n = len(pieces)
    count, depth, width, length = base.shape
    part = pieces[0].shape[1]
    piece = pl.BlockSpec((count, part, ROWS, length), lambda i, me: (0, 0, i, 0))
    layers = pl.BlockSpec((count, n * part, ROWS, length), lambda i, me: (0, chunk, i, 0))
    return pl.pallas_call(
        functools.partial(chunk_kernel, n),
        grid_spec=pltpu.PrefetchScalarGridSpec(
            num_scalar_prefetch=1,
            grid=(width // ROWS,),
            in_specs=[piece] * n + [layers] * 2 + [pl.BlockSpec(memory_space=pl.ANY)] * len(before),
            out_specs=layers,
        ),
        out_shape=pltpu.HBM(base.shape, jnp.float32),
        input_output_aliases={n + 3: 0} if before else {},
        compiler_params=pltpu.CompilerParams(vmem_limit_bytes=VMEM),
        cost_estimate=COST,
        name="chunk_update",
    )(me, *pieces, *in_hbm(base, winv, *before))


def exchange(pieces):
    n = len(pieces) + 1
    return [
        lax.ppermute(piece, "inst", [(i, i ^ code(m, n)) for i in range(n)]) for m, piece in enumerate(pieces, 1)
    ]


def after(arrays, *first):
    return lax.optimization_barrier((arrays, first))[0]


def upward(plane):
    return lax.ppermute(plane, "space", [(i, i + 1) for i in range(lax.axis_size("space") - 1)])


def downward(plane):
    return lax.ppermute(plane, "space", [(i + 1, i) for i in range(lax.axis_size("space") - 1)])


def body(field_start, source, material, face_flags, disp_table, perm_table):
    count, depth, width, length = field_start.shape
    n = lax.axis_size("inst")
    chunks = min(CHUNKS, depth // n)
    part = depth // (chunks * n)
    me = lax.axis_index("inst")
    me_array = me.reshape(1).astype(jnp.int32)

    far = cut(me_array, field_start, n, 0, part, [1])
    near = cut(me_array, after(field_start, *far), n, 0, part, range(2, n))
    going = far + near
    there = [exchange(going)]
    start, flags, material = after((field_start, face_flags, material), *going)

    moments = (me * count + jnp.arange(count)).astype(jnp.float32)
    tide = 1.0 + 0.5 * jnp.cos(2.0 * jnp.pi * moments / NT)
    mat = spectral_blocks(me, n, count)
    kappa, speed, up, down = prep(disp_table, perm_table, tide, material, flags, start)
    below, high = upward(up), downward(down)
    start = after(start, up, down)
    for chunk in range(1, chunks):
        going = cut(me_array, start, n, chunk, part)
        there.append(exchange(going))
        start = after(start, *going)
    shared = (below, high, flags, source, kappa, speed, below)
    first = stencil(False, 0, tide, start, *shared)

    back = []
    there[0] = after(there[0], first)
    for chunk in range(chunks):
        own, *rest = apply_time(me_array, field_start, there[chunk], mat, chunk)
        back.append([own] + exchange(rest))
    for half in range(1, PARTS):
        first = stencil(False, half, tide, after(field_start, back[0][1]), *shared, before=first)
    plain, winv = first

    whole = []
    there = []
    low = high = None
    for chunk in range(chunks):
        if chunk:
            back[chunk] = after(back[chunk], high)
        done = first_update(me_array, back[chunk], plain, winv, field_start, chunk, whole)
        whole, (bottom, last), sends = done[:2], done[2:4], done[4:]
        if chunk == 0:
            high = downward(bottom)
        if chunk == chunks - 1:
            low = upward(last)
        there.append(exchange(sends))
    residual, middle = whole
    there[0] = after(there[0], low)

    back = []
    second = ()
    for chunk in range(chunks):
        own, *rest = apply_time(me_array, middle, there[chunk], mat, chunk)
        back.append([own] + exchange(rest))
        if chunk < PARTS:
            ready = there[1][0] if chunk == 0 else back[0][1]
            now = after(middle, ready)
            second = stencil(True, chunk, tide, now, low, high, face_flags, source, kappa, speed, below, winv, second)
            if chunk == 0:
                there[1] = after(there[1], *second)
    base = second[0]

    field = []
    for chunk in range(chunks - 1):
        field = [chunk_update(me_array, back[chunk], base, winv, chunk, field)]
    chunk = chunks - 1
    held = [cut(me_array, array, n, chunk, part) for array in (base, winv)]
    late = max(1, n - 2)
    for m, piece in enumerate(back[chunk][:late]):
        there = [pieces[m - 1] for pieces in held] if m else None
        field = [last_update(me_array, piece, base, winv, n, chunk, m, field[0], there)]
        if m == 0:
            held, field = after((held, field), held)
    bases, winvs = (pieces[late - 1 :] for pieces in held)
    spots = [(chunk * n, m) for m in range(late, n)]
    return (residual, final_update(me_array, back[chunk][late:], bases, winvs, n, spots, field[0]))


def solution(mesh):
    return jax.shard_map(
        body,
        mesh=mesh,
        in_specs=(
            P("inst", "space", None, None),
            P("inst", "space", None, None),
            P("space", None, None),
            P("inst", None, "space", None, None),
            P(),
            P(),
        ),
        out_specs=(P("inst", "space", None, None), P("inst", "space", None, None)),
        check_vma=False,
    )
```

```python
import functools

import jax
import jax.numpy as jnp
from jax import lax
from jax.experimental import pallas as pl
from jax.experimental.pallas import tpu as pltpu
from jax.sharding import PartitionSpec as P

NT = 32


omega_scale = 0.25
decay_rate = 0.3
relax_weight = 0.8

CHUNKS = 2
PARTS = 2
SUB = 8
VMEM = 20 << 20
COST = pl.CostEstimate(flops=1 << 10, bytes_accessed=1 << 10, transcendentals=0)


def code(m, n):
    return (n - m) % n


def spectral_blocks(me, n, count):
    spots = jnp.arange(NT)
    moments = (me ^ code(spots // count, n)) * count + spots % count
    diff = moments[:, None] - moments[None, :]
    angle = jnp.pi * diff.astype(jnp.float32) / NT
    parity = 1.0 - 2.0 * (diff % 2).astype(jnp.float32)
    safe = jnp.where(diff == 0, 1.0, jnp.sin(angle))
    dmat = omega_scale * jnp.where(diff == 0, 0.0, 0.5 * parity * jnp.cos(angle) / safe)
    rows = jnp.repeat(jnp.repeat(dmat, SUB, 0), SUB, 1)
    lane = jnp.arange(NT * SUB) % SUB
    return jnp.where(lane[:, None] == lane[None, :], rows, 0.0)


def in_hbm(*arrays):
    return [pltpu.with_memory_space_constraint(array, pltpu.HBM) for array in arrays]


def cut_kernel(me_ref, *refs):
    half = len(refs) // 2
    for source, out in zip(refs[:half], refs[half:]):
        out[...] = source[...]


def cut(me, field, n, chunk, part, partners=None):
    count, depth, width, length = field.shape
    partners = range(1, n) if partners is None else partners

    def block(m):
        return pl.BlockSpec(
            (count, part, width, length), lambda i, me: (0, chunk * n + (me[0] ^ code(m, n)), 0, 0)
        )

    piece = pl.BlockSpec((count, part, width, length), lambda i, me: (0, 0, 0, 0))
    return pl.pallas_call(
        cut_kernel,
        grid_spec=pltpu.PrefetchScalarGridSpec(
            num_scalar_prefetch=1,
            grid=(1,),
            in_specs=[block(m) for m in partners],
            out_specs=[piece] * len(partners),
        ),
        out_shape=[jax.ShapeDtypeStruct((count, part, width, length), jnp.float32)] * len(partners),
        compiler_params=pltpu.CompilerParams(vmem_limit_bytes=VMEM),
        cost_estimate=COST,
        name="cut",
    )(me, *in_hbm(*[field] * len(partners)))


def prep_kernel(
    disp_ref, perm_ref, tide_ref, material_ref, flags_ref, bottom_ref, last_ref, kappa_ref, speed_ref, up_ref, down_ref
):
    depth = material_ref.shape[0]
    count = flags_ref.shape[0]

    def layer(z, carry):
        material = material_ref[z]
        kappa = jnp.zeros(material.shape, jnp.float32)
        speed = jnp.zeros(material.shape, jnp.float32)
        for klass in range(disp_ref.shape[0]):
            here = material == klass
            kappa = jnp.where(here, disp_ref[klass], kappa)
            speed = jnp.where(here, perm_ref[klass], speed)
        kappa_ref[z] = kappa
        speed_ref[z] = speed
        return carry

    lax.fori_loop(0, depth, layer, 0)
    up_ref[2 * count] = kappa_ref[depth - 1]
    for t in range(count):
        flow = speed_ref[depth - 1] * tide_ref[t]
        up_ref[t] = last_ref[t, 0]
        up_ref[count + t] = jnp.where(flags_ref[t, 0, 0] != 0, -flow, flow)
        down_ref[t] = bottom_ref[t, 0]


def prep(disp_table, perm_table, tide, material, face_flags, field):
    count, _, depth, width, length = face_flags.shape
    smem = pl.BlockSpec(memory_space=pltpu.SMEM)
    cells = pl.BlockSpec((depth, width, length), lambda i: (0, 0, 0))
    up = (2 * count + 1, width, length)
    down = (count, width, length)
    return pl.pallas_call(
        prep_kernel,
        grid=(1,),
        in_specs=[
            smem,
            smem,
            smem,
            cells,
            pl.BlockSpec((count, 1, 1, width, length), lambda i: (0, 0, depth - 1, 0, 0)),
            pl.BlockSpec((count, 1, width, length), lambda i: (0, 0, 0, 0)),
            pl.BlockSpec((count, 1, width, length), lambda i: (0, depth - 1, 0, 0)),
        ],
        out_specs=[
            cells,
            cells,
            pl.BlockSpec(up, lambda i: (0, 0, 0)),
            pl.BlockSpec(down, lambda i: (0, 0, 0)),
        ],
        out_shape=[
            jax.ShapeDtypeStruct(material.shape, jnp.float32),
            jax.ShapeDtypeStruct(material.shape, jnp.float32),
            jax.ShapeDtypeStruct(up, jnp.float32),
            jax.ShapeDtypeStruct(down, jnp.float32),
        ],
        compiler_params=pltpu.CompilerParams(vmem_limit_bytes=VMEM),
        cost_estimate=COST,
        name="prep",
    )(disp_table, perm_table, tide, *in_hbm(material, face_flags, field, field))


def stencil_kernel(
    second, first, aliased, tide_ref, u_ref, low_ref, high_ref, flags_ref, src_ref, kappa_ref, speed_ref, below_k_ref, below_f_ref, *rest
):
    if second:
        winv_ref, out_ref = rest[0], rest[-1]
    else:
        out_ref, winv_ref = rest[aliased:]
    depth, width, length = u_ref.shape[1:]
    tide = tide_ref[first + pl.program_id(0)]
    row = lax.broadcasted_iota(jnp.int32, (width, length), 0)
    col = lax.broadcasted_iota(jnp.int32, (width, length), 1)
    last_row, last_col = row == width - 1, col == length - 1

    below_k, below_f = below_k_ref[0], below_f_ref[0]
    au_low = (below_k + jnp.maximum(below_f, 0.0)) * low_ref[0]
    b_low = below_k - jnp.minimum(below_f, 0.0)

    def layer(z, carry, u_up):
        au_low, b_low = carry
        u = u_ref[0, z]
        kappa = kappa_ref[z]
        full = kappa + speed_ref[z] * tide

        def coefs(dim):
            back = flags_ref[0, dim, z] != 0
            return jnp.where(back, kappa, full), jnp.where(back, full, kappa)

        a, b = coefs(0)
        total = b * u_up + au_low
        diag = (decay_rate + a) + b_low
        next_carry = (a * u, b)
        for dim, last in ((1, last_row), (2, last_col)):
            a, b = coefs(dim)
            size = u.shape[dim - 1]
            b = jnp.where(last, 0.0, b)
            au = jnp.where(last, 0.0, a * u)
            total = total + b * pltpu.roll(u, size - 1, dim - 1) + pltpu.roll(au, 1, dim - 1)
            if not second:
                diag = diag + (a + pltpu.roll(b, 1, dim - 1))
        if second:
            out_ref[0, z] = (1.0 - relax_weight) * u + winv_ref[0, z] * (total + src_ref[0, z])
        else:
            out_ref[0, z] = diag * u - total - src_ref[0, z]
            winv_ref[0, z] = relax_weight / diag
        return next_carry

    carry = lax.fori_loop(0, depth - 1, lambda z, c: layer(z, c, u_ref[0, z + 1]), (au_low, b_low))
    layer(depth - 1, carry, high_ref[0])


def stencil(second, part, tide, u, low, high, flags, src, kappa, speed, below, winv=None, before=()):
    count, depth, width, length = u.shape
    ends = (0, count // 2, count) if second else (0, count // 4, count)
    first, stop = ends[part : part + 2]
    field = pl.BlockSpec((1, depth, width, length), lambda t: (first + t, 0, 0, 0))
    plane = pl.BlockSpec((1, width, length), lambda t: (first + t, 0, 0))
    cells = pl.BlockSpec((depth, width, length), lambda t: (0, 0, 0))
    in_specs = [
        pl.BlockSpec(memory_space=pltpu.SMEM),
        field,
        plane,
        plane,
        pl.BlockSpec((1, 3, depth, width, length), lambda t: (first + t, 0, 0, 0, 0)),
        field,
        cells,
        cells,
        pl.BlockSpec((1, width, length), lambda t: (2 * count, 0, 0)),
        pl.BlockSpec((1, width, length), lambda t: (count + first + t, 0, 0)),
    ]
    args = [tide, *in_hbm(u), low, high, *in_hbm(flags, src), kappa, speed, below, below]
    if second:
        in_specs.append(field)
        args.extend(in_hbm(winv))
    aliases = {len(args) + i: i for i in range(len(before))}
    in_specs += [pl.BlockSpec(memory_space=pl.ANY)] * len(before)
    args.extend(in_hbm(*before))
    shape = pltpu.HBM(u.shape, jnp.float32)
    outs = 1 if second else 2
    return pl.pallas_call(
        functools.partial(stencil_kernel, second, first, len(before)),
        grid=(stop - first,),
        in_specs=in_specs,
        out_specs=[field] * outs,
        out_shape=[shape] * outs,
        input_output_aliases=aliases,
        compiler_params=pltpu.CompilerParams(vmem_limit_bytes=VMEM),
        cost_estimate=COST,
        name="stencil_two" if second else "stencil_one",
    )(*args)


def apply_kernel(n, me_ref, own_ref, *refs):
    received, mat_ref, outs = refs[: n - 1], refs[n - 1], refs[n:]
    parts = [own_ref, *received]
    count, _, width, length = own_ref.shape
    groups = width // SUB
    blocks = jnp.concatenate([part[:, 0] for part in parts], 0)
    wide = jnp.concatenate(
        [blocks[:, g * SUB : (g + 1) * SUB].reshape(NT * SUB, length) for g in range(groups)], 1
    )
    product = lax.dot_general(
        mat_ref[...],
        wide,
        (((1,), (0,)), ((), ())),
        precision=lax.Precision.HIGHEST,
        preferred_element_type=jnp.float32,
    )
    for g in range(groups):
        piece = product[:, g * length : (g + 1) * length].reshape(NT, SUB, length)
        for m, out in enumerate(outs):
            out[:, 0, g * SUB : (g + 1) * SUB] = piece[m * count : (m + 1) * count]


def apply_time(me, field, received, mat, chunk):
    n = len(received) + 1
    count, depth, width, length = field.shape
    part = received[0].shape[1]
    piece = pl.BlockSpec((count, 1, width, length), lambda i, me: (0, i, 0, 0))
    shape = jax.ShapeDtypeStruct(received[0].shape, jnp.float32)
    size = n * received[0].size
    return pl.pallas_call(
        functools.partial(apply_kernel, n),
        grid_spec=pltpu.PrefetchScalarGridSpec(
            num_scalar_prefetch=1,
            grid=(part,),
            in_specs=[
                pl.BlockSpec((count, 1, width, length), lambda i, me: (0, (chunk * n + me[0]) * part + i, 0, 0)),
                *([piece] * (n - 1)),
                pl.BlockSpec(mat.shape, lambda i, me: (0, 0)),
            ],
            out_specs=[piece] * n,
        ),
        out_shape=[shape] * n,
        compiler_params=pltpu.CompilerParams(vmem_limit_bytes=VMEM),
        cost_estimate=COST,
        name="apply_time",
    )(me, *in_hbm(field), *received, mat)


ROWS = 16


def first_kernel(n, aliased, me_ref, *refs):
    pieces, (s_ref, winv_ref, u_ref) = refs[:n], refs[n : n + 3]
    res_ref, mid_ref, first_ref, last_ref, *sends = refs[n + 3 + aliased :]
    part = pieces[0].shape[1]
    for m, piece in enumerate(pieces):
        for i in range(part):
            z = (me_ref[0] ^ code(m, n)) * part + i
            res = s_ref[:, z] + piece[:, i]
            mid = u_ref[:, z] - winv_ref[:, z] * res
            res_ref[:, z] = res
            mid_ref[:, z] = mid
            if m:
                sends[m - 1][:, i] = mid
    first_ref[...] = mid_ref[:, 0]
    last_ref[...] = mid_ref[:, n * part - 1]


def first_update(me, pieces, s, winv, u, chunk, before):
    n = len(pieces)
    count, depth, width, length = u.shape
    part = pieces[0].shape[1]
    piece = pl.BlockSpec((count, part, ROWS, length), lambda i, me: (0, 0, i, 0))
    layers = pl.BlockSpec((count, n * part, ROWS, length), lambda i, me: (0, chunk, i, 0))
    whole = pltpu.HBM(u.shape, jnp.float32)
    aliased = len(before)
    size = n * pieces[0].size
    return pl.pallas_call(
        functools.partial(first_kernel, n, aliased),
        grid_spec=pltpu.PrefetchScalarGridSpec(
            num_scalar_prefetch=1,
            grid=(width // ROWS,),
            in_specs=[piece] * n + [layers] * 3 + [pl.BlockSpec(memory_space=pl.ANY)] * aliased,
            out_specs=[layers] * 2 + [pl.BlockSpec((count, ROWS, length), lambda i, me: (0, i, 0))] * 2 + [piece] * (n - 1),
        ),
        out_shape=[whole] * 2
        + [jax.ShapeDtypeStruct((count, width, length), jnp.float32)] * 2
        + [jax.ShapeDtypeStruct(pieces[0].shape, jnp.float32)] * (n - 1),
        input_output_aliases={n + 4 + i: i for i in range(aliased)},
        compiler_params=pltpu.CompilerParams(vmem_limit_bytes=VMEM),
        cost_estimate=COST,
        name="first_update",
    )(me, *pieces, *in_hbm(s, winv, u, *before))


def last_kernel(piece_ref, base_ref, winv_ref, *refs):
    refs[-1][...] = base_ref[...] - winv_ref[...] * piece_ref[...]


def last_update(me, piece, base, winv, n, chunk, m, before, held=None):
    count, part, width, length = piece.shape
    layers = pl.BlockSpec((count, part, width, length), lambda i, me: (0, chunk * n + (me[0] ^ code(m, n)), 0, 0))
    block = pl.BlockSpec((count, part, width, length), lambda i, me: (0, 0, 0, 0))
    return pl.pallas_call(
        lambda me_ref, *refs: last_kernel(*refs),
        grid_spec=pltpu.PrefetchScalarGridSpec(
            num_scalar_prefetch=1,
            grid=(1,),
            in_specs=[block] + [block if held else layers] * 2 + [pl.BlockSpec(memory_space=pl.ANY)],
            out_specs=layers,
        ),
        out_shape=pltpu.HBM(base.shape, jnp.float32),
        input_output_aliases={4: 0},
        compiler_params=pltpu.CompilerParams(vmem_limit_bytes=VMEM),
        cost_estimate=COST,
        name="last_update",
    )(me, piece, *(held or in_hbm(base, winv)), *in_hbm(before))


def final_kernel(n, spots, me_ref, *refs):
    count = len(spots)
    pieces, bases, winvs = refs[:count], refs[count : 2 * count], refs[2 * count : 3 * count]
    out_ref, sums, sems = refs[3 * count + 1 :]
    part = pieces[0].shape[1]
    copies = []
    for p, (first, m) in enumerate(spots):
        for i in range(part):
            sums[p, :, i] = bases[p][:, i] - winvs[p][:, i] * pieces[p][:, i]
            place = (first + (me_ref[0] ^ code(m, n))) * part + i
            copy = pltpu.make_async_copy(
                sums.at[p, :, pl.ds(i, 1)], out_ref.at[:, pl.ds(place, 1)], sems.at[p, i]
            )
            copy.start()
            copies.append(copy)
    for copy in copies:
        copy.wait()


def final_update(me, pieces, bases, winvs, n, spots, before):
    vmem = pl.BlockSpec(memory_space=pltpu.VMEM)
    anywhere = pl.BlockSpec(memory_space=pl.ANY)
    count = len(pieces)
    return pl.pallas_call(
        functools.partial(final_kernel, n, spots),
        in_specs=[pl.BlockSpec(memory_space=pltpu.SMEM)] + [vmem] * (3 * count) + [anywhere],
        out_specs=anywhere,
        out_shape=pltpu.HBM(before.shape, jnp.float32),
        scratch_shapes=[
            pltpu.VMEM((count, *pieces[0].shape), jnp.float32),
            pltpu.SemaphoreType.DMA((count, pieces[0].shape[1])),
        ],
        input_output_aliases={3 * count + 1: 0},
        compiler_params=pltpu.CompilerParams(vmem_limit_bytes=VMEM),
        cost_estimate=COST,
        name="final_update",
    )(me, *pieces, *bases, *winvs, *in_hbm(before))


def chunk_kernel(n, me_ref, *refs):
    pieces, (base_ref, winv_ref) = refs[:n], refs[n : n + 2]
    out_ref = refs[-1]
    part = pieces[0].shape[1]
    for m, piece in enumerate(pieces):
        for i in range(part):
            z = (me_ref[0] ^ code(m, n)) * part + i
            out_ref[:, z] = base_ref[:, z] - winv_ref[:, z] * piece[:, i]


def chunk_update(me, pieces, base, winv, chunk, before):
    n = len(pieces)
    count, depth, width, length = base.shape
    part = pieces[0].shape[1]
    piece = pl.BlockSpec((count, part, ROWS, length), lambda i, me: (0, 0, i, 0))
    layers = pl.BlockSpec((count, n * part, ROWS, length), lambda i, me: (0, chunk, i, 0))
    return pl.pallas_call(
        functools.partial(chunk_kernel, n),
        grid_spec=pltpu.PrefetchScalarGridSpec(
            num_scalar_prefetch=1,
            grid=(width // ROWS,),
            in_specs=[piece] * n + [layers] * 2 + [pl.BlockSpec(memory_space=pl.ANY)] * len(before),
            out_specs=layers,
        ),
        out_shape=pltpu.HBM(base.shape, jnp.float32),
        input_output_aliases={n + 3: 0} if before else {},
        compiler_params=pltpu.CompilerParams(vmem_limit_bytes=VMEM),
        cost_estimate=COST,
        name="chunk_update",
    )(me, *pieces, *in_hbm(base, winv, *before))


def exchange(pieces):
    n = len(pieces) + 1
    return [
        lax.ppermute(piece, "inst", [(i, i ^ code(m, n)) for i in range(n)]) for m, piece in enumerate(pieces, 1)
    ]


def after(arrays, *first):
    return lax.optimization_barrier((arrays, first))[0]


def upward(plane):
    return lax.ppermute(plane, "space", [(i, i + 1) for i in range(lax.axis_size("space") - 1)])


def downward(plane):
    return lax.ppermute(plane, "space", [(i + 1, i) for i in range(lax.axis_size("space") - 1)])


def body(field_start, source, material, face_flags, disp_table, perm_table):
    count, depth, width, length = field_start.shape
    n = lax.axis_size("inst")
    chunks = min(CHUNKS, depth // n)
    part = depth // (chunks * n)
    me = lax.axis_index("inst")
    me_array = me.reshape(1).astype(jnp.int32)

    far = cut(me_array, field_start, n, 0, part, [1])
    near = cut(me_array, after(field_start, *far), n, 0, part, range(2, n))
    going = far + near
    there = [exchange(going)]
    start, flags, material = after((field_start, face_flags, material), *going)

    moments = (me * count + jnp.arange(count)).astype(jnp.float32)
    tide = 1.0 + 0.5 * jnp.cos(2.0 * jnp.pi * moments / NT)
    mat = spectral_blocks(me, n, count)
    kappa, speed, up, down = prep(disp_table, perm_table, tide, material, flags, start)
    below, high = upward(up), downward(down)
    start = after(start, up, down)
    for chunk in range(1, chunks):
        going = cut(me_array, start, n, chunk, part)
        there.append(exchange(going))
        start = after(start, *going)
    shared = (below, high, flags, source, kappa, speed, below)
    first = stencil(False, 0, tide, start, *shared)

    back = []
    there[0] = after(there[0], first)
    for chunk in range(chunks):
        own, *rest = apply_time(me_array, field_start, there[chunk], mat, chunk)
        back.append([own] + exchange(rest))
    for half in range(1, PARTS):
        first = stencil(False, half, tide, after(field_start, back[0][1]), *shared, before=first)
    plain, winv = first

    whole = []
    there = []
    low = high = None
    for chunk in range(chunks):
        if chunk:
            back[chunk] = after(back[chunk], high)
        done = first_update(me_array, back[chunk], plain, winv, field_start, chunk, whole)
        whole, (bottom, last), sends = done[:2], done[2:4], done[4:]
        if chunk == 0:
            high = downward(bottom)
        if chunk == chunks - 1:
            low = upward(last)
        there.append(exchange(sends))
    residual, middle = whole
    there[0] = after(there[0], low)

    back = []
    second = ()
    for chunk in range(chunks):
        own, *rest = apply_time(me_array, middle, there[chunk], mat, chunk)
        back.append([own] + exchange(rest))
        if chunk < PARTS:
            ready = there[1][0] if chunk == 0 else back[0][1]
            now = after(middle, ready)
            second = stencil(True, chunk, tide, now, low, high, face_flags, source, kappa, speed, below, winv, second)
            if chunk == 0:
                there[1] = after(there[1], *second)
    base = second[0]

    field = []
    for chunk in range(chunks - 1):
        field = [chunk_update(me_array, back[chunk], base, winv, chunk, field)]
    chunk = chunks - 1
    held = [cut(me_array, array, n, chunk, part) for array in (base, winv)]
    late = max(1, n - 2)
    for m, piece in enumerate(back[chunk][:late]):
        there = [pieces[m - 1] for pieces in held] if m else None
        field = [last_update(me_array, piece, base, winv, n, chunk, m, field[0], there)]
        if m == 0:
            held, field = after((held, field), held)
    bases, winvs = (pieces[late - 1 :] for pieces in held)
    spots = [(chunk * n, m) for m in range(late, n)]
    return (residual, final_update(me_array, back[chunk][late:], bases, winvs, n, spots, field[0]))


def solution(mesh):
    return jax.shard_map(
        body,
        mesh=mesh,
        in_specs=(
            P("inst", "space", None, None),
            P("inst", "space", None, None),
            P("space", None, None),
            P("inst", None, "space", None, None),
            P(),
            P(),
        ),
        out_specs=(P("inst", "space", None, None), P("inst", "space", None, None)),
        check_vma=False,
    )
```

```python
import functools

import jax
import jax.numpy as jnp
from jax import lax
from jax.experimental import pallas as pl
from jax.experimental.pallas import tpu as pltpu
from jax.sharding import PartitionSpec as P

NT = 32


omega_scale = 0.25
decay_rate = 0.3
relax_weight = 0.8

CHUNKS = 2
PARTS = 2
SUB = 8
VMEM = 20 << 20
COST = pl.CostEstimate(flops=1 << 10, bytes_accessed=1 << 10, transcendentals=0)


def code(m, n):
    return (n - m) % n


def spectral_blocks(me, n, count):
    spots = jnp.arange(NT)
    moments = (me ^ code(spots // count, n)) * count + spots % count
    diff = moments[:, None] - moments[None, :]
    angle = jnp.pi * diff.astype(jnp.float32) / NT
    parity = 1.0 - 2.0 * (diff % 2).astype(jnp.float32)
    safe = jnp.where(diff == 0, 1.0, jnp.sin(angle))
    dmat = omega_scale * jnp.where(diff == 0, 0.0, 0.5 * parity * jnp.cos(angle) / safe)
    rows = jnp.repeat(jnp.repeat(dmat, SUB, 0), SUB, 1)
    lane = jnp.arange(NT * SUB) % SUB
    return jnp.where(lane[:, None] == lane[None, :], rows, 0.0)


def in_hbm(*arrays):
    return [pltpu.with_memory_space_constraint(array, pltpu.HBM) for array in arrays]


def cut_kernel(me_ref, *refs):
    half = len(refs) // 2
    for source, out in zip(refs[:half], refs[half:]):
        out[...] = source[...]


def cut(me, field, n, chunk, part, partners=None):
    count, depth, width, length = field.shape
    partners = range(1, n) if partners is None else partners

    def block(m):
        return pl.BlockSpec(
            (count, part, width, length), lambda i, me: (0, chunk * n + (me[0] ^ code(m, n)), 0, 0)
        )

    piece = pl.BlockSpec((count, part, width, length), lambda i, me: (0, 0, 0, 0))
    return pl.pallas_call(
        cut_kernel,
        grid_spec=pltpu.PrefetchScalarGridSpec(
            num_scalar_prefetch=1,
            grid=(1,),
            in_specs=[block(m) for m in partners],
            out_specs=[piece] * len(partners),
        ),
        out_shape=[jax.ShapeDtypeStruct((count, part, width, length), jnp.float32)] * len(partners),
        compiler_params=pltpu.CompilerParams(vmem_limit_bytes=VMEM),
        cost_estimate=COST,
        name="cut",
    )(me, *in_hbm(*[field] * len(partners)))


def prep_kernel(
    disp_ref, perm_ref, tide_ref, material_ref, flags_ref, bottom_ref, last_ref, kappa_ref, speed_ref, up_ref, down_ref
):
    depth = material_ref.shape[0]
    count = flags_ref.shape[0]

    def layer(z, carry):
        material = material_ref[z]
        kappa = jnp.zeros(material.shape, jnp.float32)
        speed = jnp.zeros(material.shape, jnp.float32)
        for klass in range(disp_ref.shape[0]):
            here = material == klass
            kappa = jnp.where(here, disp_ref[klass], kappa)
            speed = jnp.where(here, perm_ref[klass], speed)
        kappa_ref[z] = kappa
        speed_ref[z] = speed
        return carry

    lax.fori_loop(0, depth, layer, 0)
    up_ref[2 * count] = kappa_ref[depth - 1]
    for t in range(count):
        flow = speed_ref[depth - 1] * tide_ref[t]
        up_ref[t] = last_ref[t, 0]
        up_ref[count + t] = jnp.where(flags_ref[t, 0, 0] != 0, -flow, flow)
        down_ref[t] = bottom_ref[t, 0]


def prep(disp_table, perm_table, tide, material, face_flags, field):
    count, _, depth, width, length = face_flags.shape
    smem = pl.BlockSpec(memory_space=pltpu.SMEM)
    cells = pl.BlockSpec((depth, width, length), lambda i: (0, 0, 0))
    up = (2 * count + 1, width, length)
    down = (count, width, length)
    return pl.pallas_call(
        prep_kernel,
        grid=(1,),
        in_specs=[
            smem,
            smem,
            smem,
            cells,
            pl.BlockSpec((count, 1, 1, width, length), lambda i: (0, 0, depth - 1, 0, 0)),
            pl.BlockSpec((count, 1, width, length), lambda i: (0, 0, 0, 0)),
            pl.BlockSpec((count, 1, width, length), lambda i: (0, depth - 1, 0, 0)),
        ],
        out_specs=[
            cells,
            cells,
            pl.BlockSpec(up, lambda i: (0, 0, 0)),
            pl.BlockSpec(down, lambda i: (0, 0, 0)),
        ],
        out_shape=[
            jax.ShapeDtypeStruct(material.shape, jnp.float32),
            jax.ShapeDtypeStruct(material.shape, jnp.float32),
            jax.ShapeDtypeStruct(up, jnp.float32),
            jax.ShapeDtypeStruct(down, jnp.float32),
        ],
        compiler_params=pltpu.CompilerParams(vmem_limit_bytes=VMEM),
        cost_estimate=COST,
        name="prep",
    )(disp_table, perm_table, tide, *in_hbm(material, face_flags, field, field))


def stencil_kernel(
    second, first, aliased, tide_ref, u_ref, low_ref, high_ref, flags_ref, src_ref, kappa_ref, speed_ref, below_k_ref, below_f_ref, *rest
):
    if second:
        winv_ref, out_ref = rest[0], rest[-1]
    else:
        out_ref, winv_ref = rest[aliased:]
    depth, width, length = u_ref.shape[1:]
    tide = tide_ref[first + pl.program_id(0)]
    row = lax.broadcasted_iota(jnp.int32, (width, length), 0)
    col = lax.broadcasted_iota(jnp.int32, (width, length), 1)
    last_row, last_col = row == width - 1, col == length - 1

    below_k, below_f = below_k_ref[0], below_f_ref[0]
    au_low = (below_k + jnp.maximum(below_f, 0.0)) * low_ref[0]
    b_low = below_k - jnp.minimum(below_f, 0.0)

    def layer(z, carry, u_up):
        au_low, b_low = carry
        u = u_ref[0, z]
        kappa = kappa_ref[z]
        full = kappa + speed_ref[z] * tide

        def coefs(dim):
            back = flags_ref[0, dim, z] != 0
            return jnp.where(back, kappa, full), jnp.where(back, full, kappa)

        a, b = coefs(0)
        total = b * u_up + au_low
        diag = (decay_rate + a) + b_low
        next_carry = (a * u, b)
        for dim, last in ((1, last_row), (2, last_col)):
            a, b = coefs(dim)
            size = u.shape[dim - 1]
            b = jnp.where(last, 0.0, b)
            au = jnp.where(last, 0.0, a * u)
            total = total + b * pltpu.roll(u, size - 1, dim - 1) + pltpu.roll(au, 1, dim - 1)
            if not second:
                diag = diag + (a + pltpu.roll(b, 1, dim - 1))
        if second:
            out_ref[0, z] = (1.0 - relax_weight) * u + winv_ref[0, z] * (total + src_ref[0, z])
        else:
            out_ref[0, z] = diag * u - total - src_ref[0, z]
            winv_ref[0, z] = relax_weight / diag
        return next_carry

    carry = lax.fori_loop(0, depth - 1, lambda z, c: layer(z, c, u_ref[0, z + 1]), (au_low, b_low))
    layer(depth - 1, carry, high_ref[0])


def stencil(second, part, tide, u, low, high, flags, src, kappa, speed, below, winv=None, before=()):
    count, depth, width, length = u.shape
    ends = (0, count // 2, count) if second else (0, count // 4, count)
    first, stop = ends[part : part + 2]
    field = pl.BlockSpec((1, depth, width, length), lambda t: (first + t, 0, 0, 0))
    plane = pl.BlockSpec((1, width, length), lambda t: (first + t, 0, 0))
    cells = pl.BlockSpec((depth, width, length), lambda t: (0, 0, 0))
    in_specs = [
        pl.BlockSpec(memory_space=pltpu.SMEM),
        field,
        plane,
        plane,
        pl.BlockSpec((1, 3, depth, width, length), lambda t: (first + t, 0, 0, 0, 0)),
        field,
        cells,
        cells,
        pl.BlockSpec((1, width, length), lambda t: (2 * count, 0, 0)),
        pl.BlockSpec((1, width, length), lambda t: (count + first + t, 0, 0)),
    ]
    args = [tide, *in_hbm(u), low, high, *in_hbm(flags, src), kappa, speed, below, below]
    if second:
        in_specs.append(field)
        args.extend(in_hbm(winv))
    aliases = {len(args) + i: i for i in range(len(before))}
    in_specs += [pl.BlockSpec(memory_space=pl.ANY)] * len(before)
    args.extend(in_hbm(*before))
    shape = pltpu.HBM(u.shape, jnp.float32)
    outs = 1 if second else 2
    return pl.pallas_call(
        functools.partial(stencil_kernel, second, first, len(before)),
        grid=(stop - first,),
        in_specs=in_specs,
        out_specs=[field] * outs,
        out_shape=[shape] * outs,
        input_output_aliases=aliases,
        compiler_params=pltpu.CompilerParams(vmem_limit_bytes=VMEM),
        cost_estimate=COST,
        name="stencil_two" if second else "stencil_one",
    )(*args)


def apply_kernel(n, me_ref, own_ref, *refs):
    received, mat_ref, outs = refs[: n - 1], refs[n - 1], refs[n:]
    parts = [own_ref, *received]
    count, _, width, length = own_ref.shape
    groups = width // SUB
    blocks = jnp.concatenate([part[:, 0] for part in parts], 0)
    wide = jnp.concatenate(
        [blocks[:, g * SUB : (g + 1) * SUB].reshape(NT * SUB, length) for g in range(groups)], 1
    )
    product = lax.dot_general(
        mat_ref[...],
        wide,
        (((1,), (0,)), ((), ())),
        precision=lax.Precision.HIGHEST,
        preferred_element_type=jnp.float32,
    )
    for g in range(groups):
        piece = product[:, g * length : (g + 1) * length].reshape(NT, SUB, length)
        for m, out in enumerate(outs):
            out[:, 0, g * SUB : (g + 1) * SUB] = piece[m * count : (m + 1) * count]


def apply_time(me, field, received, mat, chunk):
    n = len(received) + 1
    count, depth, width, length = field.shape
    part = received[0].shape[1]
    piece = pl.BlockSpec((count, 1, width, length), lambda i, me: (0, i, 0, 0))
    shape = jax.ShapeDtypeStruct(received[0].shape, jnp.float32)
    size = n * received[0].size
    return pl.pallas_call(
        functools.partial(apply_kernel, n),
        grid_spec=pltpu.PrefetchScalarGridSpec(
            num_scalar_prefetch=1,
            grid=(part,),
            in_specs=[
                pl.BlockSpec((count, 1, width, length), lambda i, me: (0, (chunk * n + me[0]) * part + i, 0, 0)),
                *([piece] * (n - 1)),
                pl.BlockSpec(mat.shape, lambda i, me: (0, 0)),
            ],
            out_specs=[piece] * n,
        ),
        out_shape=[shape] * n,
        compiler_params=pltpu.CompilerParams(vmem_limit_bytes=VMEM),
        cost_estimate=COST,
        name="apply_time",
    )(me, *in_hbm(field), *received, mat)


ROWS = 16


def first_kernel(n, aliased, me_ref, *refs):
    pieces, (s_ref, winv_ref, u_ref) = refs[:n], refs[n : n + 3]
    res_ref, mid_ref, first_ref, last_ref, *sends = refs[n + 3 + aliased :]
    part = pieces[0].shape[1]
    for m, piece in enumerate(pieces):
        for i in range(part):
            z = (me_ref[0] ^ code(m, n)) * part + i
            res = s_ref[:, z] + piece[:, i]
            mid = u_ref[:, z] - winv_ref[:, z] * res
            res_ref[:, z] = res
            mid_ref[:, z] = mid
            if m:
                sends[m - 1][:, i] = mid
    first_ref[...] = mid_ref[:, 0]
    last_ref[...] = mid_ref[:, n * part - 1]


def first_update(me, pieces, s, winv, u, chunk, before):
    n = len(pieces)
    count, depth, width, length = u.shape
    part = pieces[0].shape[1]
    piece = pl.BlockSpec((count, part, ROWS, length), lambda i, me: (0, 0, i, 0))
    layers = pl.BlockSpec((count, n * part, ROWS, length), lambda i, me: (0, chunk, i, 0))
    whole = pltpu.HBM(u.shape, jnp.float32)
    aliased = len(before)
    size = n * pieces[0].size
    return pl.pallas_call(
        functools.partial(first_kernel, n, aliased),
        grid_spec=pltpu.PrefetchScalarGridSpec(
            num_scalar_prefetch=1,
            grid=(width // ROWS,),
            in_specs=[piece] * n + [layers] * 3 + [pl.BlockSpec(memory_space=pl.ANY)] * aliased,
            out_specs=[layers] * 2 + [pl.BlockSpec((count, ROWS, length), lambda i, me: (0, i, 0))] * 2 + [piece] * (n - 1),
        ),
        out_shape=[whole] * 2
        + [jax.ShapeDtypeStruct((count, width, length), jnp.float32)] * 2
        + [jax.ShapeDtypeStruct(pieces[0].shape, jnp.float32)] * (n - 1),
        input_output_aliases={n + 4 + i: i for i in range(aliased)},
        compiler_params=pltpu.CompilerParams(vmem_limit_bytes=VMEM),
        cost_estimate=COST,
        name="first_update",
    )(me, *pieces, *in_hbm(s, winv, u, *before))


def last_kernel(piece_ref, base_ref, winv_ref, *refs):
    refs[-1][...] = base_ref[...] - winv_ref[...] * piece_ref[...]


def last_update(me, piece, base, winv, n, chunk, m, before, held=None):
    count, part, width, length = piece.shape
    layers = pl.BlockSpec((count, part, width, length), lambda i, me: (0, chunk * n + (me[0] ^ code(m, n)), 0, 0))
    block = pl.BlockSpec((count, part, width, length), lambda i, me: (0, 0, 0, 0))
    return pl.pallas_call(
        lambda me_ref, *refs: last_kernel(*refs),
        grid_spec=pltpu.PrefetchScalarGridSpec(
            num_scalar_prefetch=1,
            grid=(1,),
            in_specs=[block] + [block if held else layers] * 2 + [pl.BlockSpec(memory_space=pl.ANY)],
            out_specs=layers,
        ),
        out_shape=pltpu.HBM(base.shape, jnp.float32),
        input_output_aliases={4: 0},
        compiler_params=pltpu.CompilerParams(vmem_limit_bytes=VMEM),
        cost_estimate=COST,
        name="last_update",
    )(me, piece, *(held or in_hbm(base, winv)), *in_hbm(before))


def final_kernel(n, spots, me_ref, *refs):
    count = len(spots)
    pieces, bases, winvs = refs[:count], refs[count : 2 * count], refs[2 * count : 3 * count]
    out_ref, sums, sems = refs[3 * count + 1 :]
    part = pieces[0].shape[1]
    copies = []
    for p, (first, m) in enumerate(spots):
        for i in range(part):
            sums[p, :, i] = bases[p][:, i] - winvs[p][:, i] * pieces[p][:, i]
            place = (first + (me_ref[0] ^ code(m, n))) * part + i
            copy = pltpu.make_async_copy(
                sums.at[p, :, pl.ds(i, 1)], out_ref.at[:, pl.ds(place, 1)], sems.at[p, i]
            )
            copy.start()
            copies.append(copy)
    for copy in copies:
        copy.wait()


def final_update(me, pieces, bases, winvs, n, spots, before):
    vmem = pl.BlockSpec(memory_space=pltpu.VMEM)
    anywhere = pl.BlockSpec(memory_space=pl.ANY)
    count = len(pieces)
    return pl.pallas_call(
        functools.partial(final_kernel, n, spots),
        in_specs=[pl.BlockSpec(memory_space=pltpu.SMEM)] + [vmem] * (3 * count) + [anywhere],
        out_specs=anywhere,
        out_shape=pltpu.HBM(before.shape, jnp.float32),
        scratch_shapes=[
            pltpu.VMEM((count, *pieces[0].shape), jnp.float32),
            pltpu.SemaphoreType.DMA((count, pieces[0].shape[1])),
        ],
        input_output_aliases={3 * count + 1: 0},
        compiler_params=pltpu.CompilerParams(vmem_limit_bytes=VMEM),
        cost_estimate=COST,
        name="final_update",
    )(me, *pieces, *bases, *winvs, *in_hbm(before))


def chunk_kernel(n, me_ref, *refs):
    pieces, (base_ref, winv_ref) = refs[:n], refs[n : n + 2]
    out_ref = refs[-1]
    part = pieces[0].shape[1]
    for m, piece in enumerate(pieces):
        for i in range(part):
            z = (me_ref[0] ^ code(m, n)) * part + i
            out_ref[:, z] = base_ref[:, z] - winv_ref[:, z] * piece[:, i]


def chunk_update(me, pieces, base, winv, chunk, before):
    n = len(pieces)
    count, depth, width, length = base.shape
    part = pieces[0].shape[1]
    piece = pl.BlockSpec((count, part, ROWS, length), lambda i, me: (0, 0, i, 0))
    layers = pl.BlockSpec((count, n * part, ROWS, length), lambda i, me: (0, chunk, i, 0))
    return pl.pallas_call(
        functools.partial(chunk_kernel, n),
        grid_spec=pltpu.PrefetchScalarGridSpec(
            num_scalar_prefetch=1,
            grid=(width // ROWS,),
            in_specs=[piece] * n + [layers] * 2 + [pl.BlockSpec(memory_space=pl.ANY)] * len(before),
            out_specs=layers,
        ),
        out_shape=pltpu.HBM(base.shape, jnp.float32),
        input_output_aliases={n + 3: 0} if before else {},
        compiler_params=pltpu.CompilerParams(vmem_limit_bytes=VMEM),
        cost_estimate=COST,
        name="chunk_update",
    )(me, *pieces, *in_hbm(base, winv, *before))


def exchange(pieces):
    n = len(pieces) + 1
    return [
        lax.ppermute(piece, "inst", [(i, i ^ code(m, n)) for i in range(n)]) for m, piece in enumerate(pieces, 1)
    ]


def after(arrays, *first):
    return lax.optimization_barrier((arrays, first))[0]


def upward(plane):
    return lax.ppermute(plane, "space", [(i, i + 1) for i in range(lax.axis_size("space") - 1)])


def downward(plane):
    return lax.ppermute(plane, "space", [(i + 1, i) for i in range(lax.axis_size("space") - 1)])


def body(field_start, source, material, face_flags, disp_table, perm_table):
    count, depth, width, length = field_start.shape
    n = lax.axis_size("inst")
    chunks = min(CHUNKS, depth // n)
    part = depth // (chunks * n)
    me = lax.axis_index("inst")
    me_array = me.reshape(1).astype(jnp.int32)

    far = cut(me_array, field_start, n, 0, part, [1])
    near = cut(me_array, after(field_start, *far), n, 0, part, range(2, n))
    going = far + near
    there = [exchange(going)]
    start, flags, material = after((field_start, face_flags, material), *going)

    moments = (me * count + jnp.arange(count)).astype(jnp.float32)
    tide = 1.0 + 0.5 * jnp.cos(2.0 * jnp.pi * moments / NT)
    mat = spectral_blocks(me, n, count)
    kappa, speed, up, down = prep(disp_table, perm_table, tide, material, flags, start)
    below, high = upward(up), downward(down)
    start = after(start, below, high)
    for chunk in range(1, chunks):
        going = cut(me_array, start, n, chunk, part)
        there.append(exchange(going))
        start = after(start, *going)
    shared = (below, high, flags, source, kappa, speed, below)
    first = stencil(False, 0, tide, start, *shared)

    back = []
    there[0] = after(there[0], first)
    for chunk in range(chunks):
        own, *rest = apply_time(me_array, field_start, there[chunk], mat, chunk)
        back.append([own] + exchange(rest))
    for half in range(1, PARTS):
        first = stencil(False, half, tide, after(field_start, back[0][1]), *shared, before=first)
    plain, winv = first

    whole = []
    there = []
    low = high = None
    for chunk in range(chunks):
        if chunk:
            back[chunk] = after(back[chunk], high)
        done = first_update(me_array, back[chunk], plain, winv, field_start, chunk, whole)
        whole, (bottom, last), sends = done[:2], done[2:4], done[4:]
        if chunk == 0:
            high = downward(bottom)
        if chunk == chunks - 1:
            low = upward(last)
        there.append(exchange(sends))
    residual, middle = whole
    there[0] = after(there[0], low)

    back = []
    second = ()
    for chunk in range(chunks):
        own, *rest = apply_time(me_array, middle, there[chunk], mat, chunk)
        back.append([own] + exchange(rest))
        if chunk < PARTS:
            ready = there[1][0] if chunk == 0 else back[0][1]
            now = after(middle, ready)
            second = stencil(True, chunk, tide, now, low, high, face_flags, source, kappa, speed, below, winv, second)
            if chunk == 0:
                there[1] = after(there[1], *second)
    base = second[0]

    field = []
    for chunk in range(chunks - 1):
        field = [chunk_update(me_array, back[chunk], base, winv, chunk, field)]
    chunk = chunks - 1
    held = [cut(me_array, array, n, chunk, part) for array in (base, winv)]
    late = max(1, n - 2)
    for m, piece in enumerate(back[chunk][:late]):
        there = [pieces[m - 1] for pieces in held] if m else None
        field = [last_update(me_array, piece, base, winv, n, chunk, m, field[0], there)]
        if m == 0:
            held, field = after((held, field), held)
    bases, winvs = (pieces[late - 1 :] for pieces in held)
    spots = [(chunk * n, m) for m in range(late, n)]
    return (residual, final_update(me_array, back[chunk][late:], bases, winvs, n, spots, field[0]))


def solution(mesh):
    return jax.shard_map(
        body,
        mesh=mesh,
        in_specs=(
            P("inst", "space", None, None),
            P("inst", "space", None, None),
            P("space", None, None),
            P("inst", None, "space", None, None),
            P(),
            P(),
        ),
        out_specs=(P("inst", "space", None, None), P("inst", "space", None, None)),
        check_vma=False,
    )
```

```python
import functools

import jax
import jax.numpy as jnp
from jax import lax
from jax.experimental import pallas as pl
from jax.experimental.pallas import tpu as pltpu
from jax.sharding import PartitionSpec as P

NT = 32


omega_scale = 0.25
decay_rate = 0.3
relax_weight = 0.8

CHUNKS = 2
PARTS = 2
SUB = 8
VMEM = 20 << 20
COST = pl.CostEstimate(flops=1 << 10, bytes_accessed=1 << 10, transcendentals=0)


def code(m, n):
    return (n - m) % n


def spectral_blocks(me, n, count):
    spots = jnp.arange(NT)
    moments = (me ^ code(spots // count, n)) * count + spots % count
    diff = moments[:, None] - moments[None, :]
    angle = jnp.pi * diff.astype(jnp.float32) / NT
    parity = 1.0 - 2.0 * (diff % 2).astype(jnp.float32)
    safe = jnp.where(diff == 0, 1.0, jnp.sin(angle))
    dmat = omega_scale * jnp.where(diff == 0, 0.0, 0.5 * parity * jnp.cos(angle) / safe)
    rows = jnp.repeat(jnp.repeat(dmat, SUB, 0), SUB, 1)
    lane = jnp.arange(NT * SUB) % SUB
    return jnp.where(lane[:, None] == lane[None, :], rows, 0.0)


def in_hbm(*arrays):
    return [pltpu.with_memory_space_constraint(array, pltpu.HBM) for array in arrays]


def cut_kernel(me_ref, *refs):
    half = len(refs) // 2
    for source, out in zip(refs[:half], refs[half:]):
        out[...] = source[...]


def cut(me, field, n, chunk, part, partners=None):
    count, depth, width, length = field.shape
    partners = range(1, n) if partners is None else partners

    def block(m):
        return pl.BlockSpec(
            (count, part, width, length), lambda i, me: (0, chunk * n + (me[0] ^ code(m, n)), 0, 0)
        )

    piece = pl.BlockSpec((count, part, width, length), lambda i, me: (0, 0, 0, 0))
    return pl.pallas_call(
        cut_kernel,
        grid_spec=pltpu.PrefetchScalarGridSpec(
            num_scalar_prefetch=1,
            grid=(1,),
            in_specs=[block(m) for m in partners],
            out_specs=[piece] * len(partners),
        ),
        out_shape=[jax.ShapeDtypeStruct((count, part, width, length), jnp.float32)] * len(partners),
        compiler_params=pltpu.CompilerParams(vmem_limit_bytes=VMEM),
        cost_estimate=COST,
        name="cut",
    )(me, *in_hbm(*[field] * len(partners)))


def prep_kernel(
    disp_ref, perm_ref, tide_ref, material_ref, flags_ref, bottom_ref, last_ref, kappa_ref, speed_ref, up_ref, down_ref
):
    depth = material_ref.shape[0]
    count = flags_ref.shape[0]

    def layer(z, carry):
        material = material_ref[z]
        kappa = jnp.zeros(material.shape, jnp.float32)
        speed = jnp.zeros(material.shape, jnp.float32)
        for klass in range(disp_ref.shape[0]):
            here = material == klass
            kappa = jnp.where(here, disp_ref[klass], kappa)
            speed = jnp.where(here, perm_ref[klass], speed)
        kappa_ref[z] = kappa
        speed_ref[z] = speed
        return carry

    lax.fori_loop(0, depth, layer, 0)
    up_ref[2 * count] = kappa_ref[depth - 1]
    for t in range(count):
        flow = speed_ref[depth - 1] * tide_ref[t]
        up_ref[t] = last_ref[t, 0]
        up_ref[count + t] = jnp.where(flags_ref[t, 0, 0] != 0, -flow, flow)
        down_ref[t] = bottom_ref[t, 0]


def prep(disp_table, perm_table, tide, material, face_flags, field):
    count, _, depth, width, length = face_flags.shape
    smem = pl.BlockSpec(memory_space=pltpu.SMEM)
    cells = pl.BlockSpec((depth, width, length), lambda i: (0, 0, 0))
    up = (2 * count + 1, width, length)
    down = (count, width, length)
    return pl.pallas_call(
        prep_kernel,
        grid=(1,),
        in_specs=[
            smem,
            smem,
            smem,
            cells,
            pl.BlockSpec((count, 1, 1, width, length), lambda i: (0, 0, depth - 1, 0, 0)),
            pl.BlockSpec((count, 1, width, length), lambda i: (0, 0, 0, 0)),
            pl.BlockSpec((count, 1, width, length), lambda i: (0, depth - 1, 0, 0)),
        ],
        out_specs=[
            cells,
            cells,
            pl.BlockSpec(up, lambda i: (0, 0, 0)),
            pl.BlockSpec(down, lambda i: (0, 0, 0)),
        ],
        out_shape=[
            jax.ShapeDtypeStruct(material.shape, jnp.float32),
            jax.ShapeDtypeStruct(material.shape, jnp.float32),
            jax.ShapeDtypeStruct(up, jnp.float32),
            jax.ShapeDtypeStruct(down, jnp.float32),
        ],
        compiler_params=pltpu.CompilerParams(vmem_limit_bytes=VMEM),
        cost_estimate=COST,
        name="prep",
    )(disp_table, perm_table, tide, *in_hbm(material, face_flags, field, field))


def stencil_kernel(
    second, first, aliased, tide_ref, u_ref, low_ref, high_ref, flags_ref, src_ref, kappa_ref, speed_ref, below_k_ref, below_f_ref, *rest
):
    if second:
        winv_ref, out_ref = rest[0], rest[-1]
    else:
        out_ref, winv_ref = rest[aliased:]
    depth, width, length = u_ref.shape[1:]
    tide = tide_ref[first + pl.program_id(0)]
    row = lax.broadcasted_iota(jnp.int32, (width, length), 0)
    col = lax.broadcasted_iota(jnp.int32, (width, length), 1)
    last_row, last_col = row == width - 1, col == length - 1

    below_k, below_f = below_k_ref[0], below_f_ref[0]
    au_low = (below_k + jnp.maximum(below_f, 0.0)) * low_ref[0]
    b_low = below_k - jnp.minimum(below_f, 0.0)

    def layer(z, carry, u_up):
        au_low, b_low = carry
        u = u_ref[0, z]
        kappa = kappa_ref[z]
        full = kappa + speed_ref[z] * tide

        def coefs(dim):
            back = flags_ref[0, dim, z] != 0
            return jnp.where(back, kappa, full), jnp.where(back, full, kappa)

        a, b = coefs(0)
        total = b * u_up + au_low
        diag = (decay_rate + a) + b_low
        next_carry = (a * u, b)
        for dim, last in ((1, last_row), (2, last_col)):
            a, b = coefs(dim)
            size = u.shape[dim - 1]
            b = jnp.where(last, 0.0, b)
            au = jnp.where(last, 0.0, a * u)
            total = total + b * pltpu.roll(u, size - 1, dim - 1) + pltpu.roll(au, 1, dim - 1)
            if not second:
                diag = diag + (a + pltpu.roll(b, 1, dim - 1))
        if second:
            out_ref[0, z] = (1.0 - relax_weight) * u + winv_ref[0, z] * (total + src_ref[0, z])
        else:
            out_ref[0, z] = diag * u - total - src_ref[0, z]
            winv_ref[0, z] = relax_weight / diag
        return next_carry

    carry = lax.fori_loop(0, depth - 1, lambda z, c: layer(z, c, u_ref[0, z + 1]), (au_low, b_low))
    layer(depth - 1, carry, high_ref[0])


def stencil(second, part, tide, u, low, high, flags, src, kappa, speed, below, winv=None, before=()):
    count, depth, width, length = u.shape
    ends = (0, count // 2, count) if second else (0, count // 4, count)
    first, stop = ends[part : part + 2]
    field = pl.BlockSpec((1, depth, width, length), lambda t: (first + t, 0, 0, 0))
    plane = pl.BlockSpec((1, width, length), lambda t: (first + t, 0, 0))
    cells = pl.BlockSpec((depth, width, length), lambda t: (0, 0, 0))
    in_specs = [
        pl.BlockSpec(memory_space=pltpu.SMEM),
        field,
        plane,
        plane,
        pl.BlockSpec((1, 3, depth, width, length), lambda t: (first + t, 0, 0, 0, 0)),
        field,
        cells,
        cells,
        pl.BlockSpec((1, width, length), lambda t: (2 * count, 0, 0)),
        pl.BlockSpec((1, width, length), lambda t: (count + first + t, 0, 0)),
    ]
    args = [tide, *in_hbm(u), low, high, *in_hbm(flags, src), kappa, speed, below, below]
    if second:
        in_specs.append(field)
        args.extend(in_hbm(winv))
    aliases = {len(args) + i: i for i in range(len(before))}
    in_specs += [pl.BlockSpec(memory_space=pl.ANY)] * len(before)
    args.extend(in_hbm(*before))
    shape = pltpu.HBM(u.shape, jnp.float32)
    outs = 1 if second else 2
    return pl.pallas_call(
        functools.partial(stencil_kernel, second, first, len(before)),
        grid=(stop - first,),
        in_specs=in_specs,
        out_specs=[field] * outs,
        out_shape=[shape] * outs,
        input_output_aliases=aliases,
        compiler_params=pltpu.CompilerParams(vmem_limit_bytes=VMEM),
        cost_estimate=COST,
        name="stencil_two" if second else "stencil_one",
    )(*args)


def apply_kernel(n, me_ref, own_ref, *refs):
    received, mat_ref, outs = refs[: n - 1], refs[n - 1], refs[n:]
    parts = [own_ref, *received]
    count, _, width, length = own_ref.shape
    groups = width // SUB
    blocks = jnp.concatenate([part[:, 0] for part in parts], 0)
    wide = jnp.concatenate(
        [blocks[:, g * SUB : (g + 1) * SUB].reshape(NT * SUB, length) for g in range(groups)], 1
    )
    product = lax.dot_general(
        mat_ref[...],
        wide,
        (((1,), (0,)), ((), ())),
        precision=lax.Precision.HIGHEST,
        preferred_element_type=jnp.float32,
    )
    for g in range(groups):
        piece = product[:, g * length : (g + 1) * length].reshape(NT, SUB, length)
        for m, out in enumerate(outs):
            out[:, 0, g * SUB : (g + 1) * SUB] = piece[m * count : (m + 1) * count]


def apply_time(me, field, received, mat, chunk):
    n = len(received) + 1
    count, depth, width, length = field.shape
    part = received[0].shape[1]
    piece = pl.BlockSpec((count, 1, width, length), lambda i, me: (0, i, 0, 0))
    shape = jax.ShapeDtypeStruct(received[0].shape, jnp.float32)
    size = n * received[0].size
    return pl.pallas_call(
        functools.partial(apply_kernel, n),
        grid_spec=pltpu.PrefetchScalarGridSpec(
            num_scalar_prefetch=1,
            grid=(part,),
            in_specs=[
                pl.BlockSpec((count, 1, width, length), lambda i, me: (0, (chunk * n + me[0]) * part + i, 0, 0)),
                *([piece] * (n - 1)),
                pl.BlockSpec(mat.shape, lambda i, me: (0, 0)),
            ],
            out_specs=[piece] * n,
        ),
        out_shape=[shape] * n,
        compiler_params=pltpu.CompilerParams(vmem_limit_bytes=VMEM),
        cost_estimate=COST,
        name="apply_time",
    )(me, *in_hbm(field), *received, mat)


ROWS = 16


def first_kernel(n, aliased, me_ref, *refs):
    pieces, (s_ref, winv_ref, u_ref) = refs[:n], refs[n : n + 3]
    res_ref, mid_ref, first_ref, last_ref, *sends = refs[n + 3 + aliased :]
    part = pieces[0].shape[1]
    for m, piece in enumerate(pieces):
        for i in range(part):
            z = (me_ref[0] ^ code(m, n)) * part + i
            res = s_ref[:, z] + piece[:, i]
            mid = u_ref[:, z] - winv_ref[:, z] * res
            res_ref[:, z] = res
            mid_ref[:, z] = mid
            if m:
                sends[m - 1][:, i] = mid
    first_ref[...] = mid_ref[:, 0]
    last_ref[...] = mid_ref[:, n * part - 1]


def first_update(me, pieces, s, winv, u, chunk, before):
    n = len(pieces)
    count, depth, width, length = u.shape
    part = pieces[0].shape[1]
    piece = pl.BlockSpec((count, part, ROWS, length), lambda i, me: (0, 0, i, 0))
    layers = pl.BlockSpec((count, n * part, ROWS, length), lambda i, me: (0, chunk, i, 0))
    whole = pltpu.HBM(u.shape, jnp.float32)
    aliased = len(before)
    size = n * pieces[0].size
    return pl.pallas_call(
        functools.partial(first_kernel, n, aliased),
        grid_spec=pltpu.PrefetchScalarGridSpec(
            num_scalar_prefetch=1,
            grid=(width // ROWS,),
            in_specs=[piece] * n + [layers] * 3 + [pl.BlockSpec(memory_space=pl.ANY)] * aliased,
            out_specs=[layers] * 2 + [pl.BlockSpec((count, ROWS, length), lambda i, me: (0, i, 0))] * 2 + [piece] * (n - 1),
        ),
        out_shape=[whole] * 2
        + [jax.ShapeDtypeStruct((count, width, length), jnp.float32)] * 2
        + [jax.ShapeDtypeStruct(pieces[0].shape, jnp.float32)] * (n - 1),
        input_output_aliases={n + 4 + i: i for i in range(aliased)},
        compiler_params=pltpu.CompilerParams(vmem_limit_bytes=VMEM),
        cost_estimate=COST,
        name="first_update",
    )(me, *pieces, *in_hbm(s, winv, u, *before))


def last_kernel(piece_ref, base_ref, winv_ref, *refs):
    refs[-1][...] = base_ref[...] - winv_ref[...] * piece_ref[...]


def last_update(me, piece, base, winv, n, chunk, m, before, held=None):
    count, part, width, length = piece.shape
    layers = pl.BlockSpec((count, part, width, length), lambda i, me: (0, chunk * n + (me[0] ^ code(m, n)), 0, 0))
    block = pl.BlockSpec((count, part, width, length), lambda i, me: (0, 0, 0, 0))
    return pl.pallas_call(
        lambda me_ref, *refs: last_kernel(*refs),
        grid_spec=pltpu.PrefetchScalarGridSpec(
            num_scalar_prefetch=1,
            grid=(1,),
            in_specs=[block] + [block if held else layers] * 2 + [pl.BlockSpec(memory_space=pl.ANY)],
            out_specs=layers,
        ),
        out_shape=pltpu.HBM(base.shape, jnp.float32),
        input_output_aliases={4: 0},
        compiler_params=pltpu.CompilerParams(vmem_limit_bytes=VMEM),
        cost_estimate=COST,
        name="last_update",
    )(me, piece, *(held or in_hbm(base, winv)), *in_hbm(before))


def final_kernel(n, spots, me_ref, *refs):
    count = len(spots)
    pieces, bases, winvs = refs[:count], refs[count : 2 * count], refs[2 * count : 3 * count]
    out_ref, sums, sems = refs[3 * count + 1 :]
    part = pieces[0].shape[1]
    copies = []
    for p, (first, m) in enumerate(spots):
        for i in range(part):
            sums[p, :, i] = bases[p][:, i] - winvs[p][:, i] * pieces[p][:, i]
            place = (first + (me_ref[0] ^ code(m, n))) * part + i
            copy = pltpu.make_async_copy(
                sums.at[p, :, pl.ds(i, 1)], out_ref.at[:, pl.ds(place, 1)], sems.at[p, i]
            )
            copy.start()
            copies.append(copy)
    for copy in copies:
        copy.wait()


def final_update(me, pieces, bases, winvs, n, spots, before):
    vmem = pl.BlockSpec(memory_space=pltpu.VMEM)
    anywhere = pl.BlockSpec(memory_space=pl.ANY)
    count = len(pieces)
    return pl.pallas_call(
        functools.partial(final_kernel, n, spots),
        in_specs=[pl.BlockSpec(memory_space=pltpu.SMEM)] + [vmem] * (3 * count) + [anywhere],
        out_specs=anywhere,
        out_shape=pltpu.HBM(before.shape, jnp.float32),
        scratch_shapes=[
            pltpu.VMEM((count, *pieces[0].shape), jnp.float32),
            pltpu.SemaphoreType.DMA((count, pieces[0].shape[1])),
        ],
        input_output_aliases={3 * count + 1: 0},
        compiler_params=pltpu.CompilerParams(vmem_limit_bytes=VMEM),
        cost_estimate=COST,
        name="final_update",
    )(me, *pieces, *bases, *winvs, *in_hbm(before))


def chunk_kernel(n, me_ref, *refs):
    pieces, (base_ref, winv_ref) = refs[:n], refs[n : n + 2]
    out_ref = refs[-1]
    part = pieces[0].shape[1]
    for m, piece in enumerate(pieces):
        for i in range(part):
            z = (me_ref[0] ^ code(m, n)) * part + i
            out_ref[:, z] = base_ref[:, z] - winv_ref[:, z] * piece[:, i]


def chunk_update(me, pieces, base, winv, chunk, before):
    n = len(pieces)
    count, depth, width, length = base.shape
    part = pieces[0].shape[1]
    piece = pl.BlockSpec((count, part, ROWS, length), lambda i, me: (0, 0, i, 0))
    layers = pl.BlockSpec((count, n * part, ROWS, length), lambda i, me: (0, chunk, i, 0))
    return pl.pallas_call(
        functools.partial(chunk_kernel, n),
        grid_spec=pltpu.PrefetchScalarGridSpec(
            num_scalar_prefetch=1,
            grid=(width // ROWS,),
            in_specs=[piece] * n + [layers] * 2 + [pl.BlockSpec(memory_space=pl.ANY)] * len(before),
            out_specs=layers,
        ),
        out_shape=pltpu.HBM(base.shape, jnp.float32),
        input_output_aliases={n + 3: 0} if before else {},
        compiler_params=pltpu.CompilerParams(vmem_limit_bytes=VMEM),
        cost_estimate=COST,
        name="chunk_update",
    )(me, *pieces, *in_hbm(base, winv, *before))


def exchange(pieces):
    n = len(pieces) + 1
    return [
        lax.ppermute(piece, "inst", [(i, i ^ code(m, n)) for i in range(n)]) for m, piece in enumerate(pieces, 1)
    ]


def after(arrays, *first):
    return lax.optimization_barrier((arrays, first))[0]


def upward(plane):
    return lax.ppermute(plane, "space", [(i, i + 1) for i in range(lax.axis_size("space") - 1)])


def downward(plane):
    return lax.ppermute(plane, "space", [(i + 1, i) for i in range(lax.axis_size("space") - 1)])


def body(field_start, source, material, face_flags, disp_table, perm_table):
    count, depth, width, length = field_start.shape
    n = lax.axis_size("inst")
    chunks = min(CHUNKS, depth // n)
    part = depth // (chunks * n)
    me = lax.axis_index("inst")
    me_array = me.reshape(1).astype(jnp.int32)

    far = cut(me_array, field_start, n, 0, part, [1])
    near = cut(me_array, after(field_start, *far), n, 0, part, range(2, n))
    going = far + near
    there = [exchange(going)]
    start, flags, material = after((field_start, face_flags, material), *going)

    moments = (me * count + jnp.arange(count)).astype(jnp.float32)
    tide = 1.0 + 0.5 * jnp.cos(2.0 * jnp.pi * moments / NT)
    mat = spectral_blocks(me, n, count)
    kappa, speed, up, down = prep(disp_table, perm_table, tide, material, flags, start)
    below, high = upward(up), downward(down)
    start = after(start, below, high)
    for chunk in range(1, chunks):
        going = cut(me_array, start, n, chunk, part)
        there.append(exchange(going))
        start = after(start, *going)
    shared = (below, high, flags, source, kappa, speed, below)
    first = stencil(False, 0, tide, start, *shared)

    back = []
    there[0] = after(there[0], first)
    for chunk in range(chunks):
        own, *rest = apply_time(me_array, field_start, there[chunk], mat, chunk)
        back.append([own] + exchange(rest))
    for half in range(1, PARTS):
        first = stencil(False, half, tide, after(field_start, back[0][1]), *shared, before=first)
    plain, winv = first

    whole = []
    there = []
    low = high = None
    for chunk in range(chunks):
        done = first_update(me_array, back[chunk], plain, winv, field_start, chunk, whole)
        whole, (bottom, last), sends = done[:2], done[2:4], done[4:]
        if chunk == 0:
            high = downward(bottom)
        if chunk == chunks - 1:
            low = upward(last)
        there.append(exchange(sends))
    residual, middle = whole
    there[0] = after(there[0], low, high)

    back = []
    second = ()
    for chunk in range(chunks):
        own, *rest = apply_time(me_array, middle, there[chunk], mat, chunk)
        back.append([own] + exchange(rest))
        if chunk < PARTS:
            ready = there[1][0] if chunk == 0 else back[0][1]
            now = after(middle, ready)
            second = stencil(True, chunk, tide, now, low, high, face_flags, source, kappa, speed, below, winv, second)
            if chunk == 0:
                there[1] = after(there[1], *second)
    base = second[0]

    field = []
    for chunk in range(chunks - 1):
        field = [chunk_update(me_array, back[chunk], base, winv, chunk, field)]
    chunk = chunks - 1
    held = [cut(me_array, array, n, chunk, part) for array in (base, winv)]
    late = max(1, n - 2)
    for m, piece in enumerate(back[chunk][:late]):
        there = [pieces[m - 1] for pieces in held] if m else None
        field = [last_update(me_array, piece, base, winv, n, chunk, m, field[0], there)]
        if m == 0:
            held, field = after((held, field), held)
    bases, winvs = (pieces[late - 1 :] for pieces in held)
    spots = [(chunk * n, m) for m in range(late, n)]
    return (residual, final_update(me_array, back[chunk][late:], bases, winvs, n, spots, field[0]))


def solution(mesh):
    return jax.shard_map(
        body,
        mesh=mesh,
        in_specs=(
            P("inst", "space", None, None),
            P("inst", "space", None, None),
            P("space", None, None),
            P("inst", None, "space", None, None),
            P(),
            P(),
        ),
        out_specs=(P("inst", "space", None, None), P("inst", "space", None, None)),
        check_vma=False,
    )
```
